256 devices in a mesh: section: 16 (over z_hi, x, core), tensor: 16 (over z_lo, y).
Axes of the slice: x: 4, y: 4, z: 8 (z_hi: 2, z_lo: 4; z = z_hi * 4 + z_lo), core: 2. Of those that a mesh axis runs over, the one named last changes fastest.
Arguments:
- entering: bfloat16 [2, 128, 4096], P(None, None, 'tensor'), may hold values from -6 to 6
- arriving: bfloat16 [16, 128, 4096], P('section', None, 'tensor'), may hold values from -6 to 6
- stashed: bfloat16 [16, 2, 128, 4096], P('section', None, None, 'tensor'), may hold values from -6 to 6
- parked: bfloat16 [16, 2, 128, 4096], P('section', None, None, 'tensor'), may hold values from -6 to 6
- evict: int32 [16, 2], P('section'), may hold values from 0 to 1, as said below
- cotangent: bfloat16 [2, 128, 4096], P(None, None, 'tensor'), may hold values from -6 to 6
- arriving_grad: bfloat16 [16, 128, 4096], P('section', None, 'tensor'), may hold values from -6 to 6
- qkv_weight: bfloat16 [16, 4096, 12288], P('section', None, 'tensor'), may hold values from -0.09375 to 0.09375
- out_weight: bfloat16 [16, 4096, 4096], P('section', 'tensor'), may hold values from -0.375 to 0.375
- norm_gain: float32 [16, 4096], P('section'), may hold values from 0.5 to 1.5
Outputs:
- section_outputs: bfloat16 [16, 2, 128, 4096], P('section', None, None, 'tensor')
- input_grads: bfloat16 [16, 2, 128, 4096], P('section', None, None, 'tensor')
- new_parked: bfloat16 [16, 2, 128, 4096], P('section', None, None, 'tensor')
The draws below stay inside these ranges and needn't reach their ends.
Inputs may be any that keep to these rules, and one draw needn't show every extreme that they name: evict[15 - s, t] and evict[s, t] may both be 1; evict[0, 0] is 1 and evict[15, 1] is 0.
All inputs are finite; a program needn't handle non-finite values.
Results may differ from the reference program's by a relative error of at most 0.035.
Values may be sent and summed in bfloat16 or wider, within the bound.
A program may use at most 64 MiB of HBM per device.

```python
import math
import jax
import jax.numpy as jnp
from jax import lax

D = 4096
HEADS = 32
HEAD_DIM = 128
SEQ = 128
TICKS = 2
SECTIONS = 16
N_TENSOR = 16


def draw_evict(key, part):
    key = jax.random.fold_in(key, 7)
    flags = jax.random.randint(key, (SECTIONS, TICKS), 0, 2, dtype=jnp.int32)
    return flags.at[0, 0].set(1).at[SECTIONS - 1, TICKS - 1].set(0)


def shard_levels(stream_key, shape, pieces, smallest, top_value):
    level, own = 1.0, jax.random.fold_in(stream_key, 6)
    for dim, blocks in pieces:
        draws = jnp.exp(jax.random.uniform(jax.random.fold_in(own, dim), (blocks,), jnp.float32, smallest / len(pieces), top_value / len(pieces)))
        level = level * jnp.repeat(draws, shape[dim] // blocks).reshape([-1 if axis == dim else 1 for axis in range(len(shape))])
    return level


def noise(own_key, shape, scale, bound, cuts=(), held_as=jnp.bfloat16):
    result = jax.random.normal(own_key, shape, jnp.float32) * scale
    if len(cuts) > 0:
        result = shard_levels(own_key, shape, cuts, -0.22, 0.18) * result
    return jnp.clip(result, min=-bound, max=bound).astype(held_as)


def setup_inputs(seed: int = 0) -> dict:
    seeds = jax.random.split(jax.random.key(seed), 11)
    entering = noise(seeds[0], (TICKS, SEQ, D), 1.0, 6.0, ((2, 16),))
    arriving = noise(seeds[1], (SECTIONS, SEQ, D), 1.0, 6.0, ((0, 16), (2, 16)))
    stashed = noise(seeds[2], (SECTIONS, TICKS, SEQ, D), 1.0, 6.0, ((0, 16), (3, 16)))
    parked = noise(seeds[3], (SECTIONS, TICKS, SEQ, D), 1.0, 6.0, ((0, 16), (3, 16)))
    evict = draw_evict(jax.random.fold_in(seeds[10], 71), 0)
    cotangent = noise(seeds[5], (TICKS, SEQ, D), 1.0, 6.0, ((2, 16),))
    arriving_grad = noise(seeds[6], (SECTIONS, SEQ, D), 1.0, 6.0, ((0, 16), (2, 16)))
    qkv_weight = noise(seeds[7], (SECTIONS, D, 3 * HEADS * HEAD_DIM), D ** -0.5, 0.09375, ((0, 16), (2, 16)))
    out_weight = noise(seeds[8], (SECTIONS, HEADS * HEAD_DIM, D), (2 * HEAD_DIM) ** -0.5, 0.375, ((0, 16), (1, 16)))
    norm_gain = jnp.clip(1.0 + 0.1 * jax.random.normal(seeds[9], (SECTIONS, D), jnp.float32), 0.5, 1.5)
    return dict(entering=entering, arriving=arriving, stashed=stashed, parked=parked, evict=evict, cotangent=cotangent, arriving_grad=arriving_grad, qkv_weight=qkv_weight, out_weight=out_weight, norm_gain=norm_gain)


def normalize(inflow):
    values = inflow.astype(jnp.float32)
    centre = lax.optimization_barrier(jnp.mean(values, axis=-1, keepdims=True))
    shifted = values - centre
    spread = lax.optimization_barrier(jnp.mean(shifted * shifted, axis=-1, keepdims=True))
    inv_scale = lax.rsqrt(spread + 1e-05)
    return (shifted * inv_scale, inv_scale)

def group_sum(left, right):
    tokens = left.shape[0]
    width = left.shape[1] // N_TENSOR
    total = jnp.zeros((tokens, right.shape[1]), jnp.float32)
    for group in range(N_TENSOR):
        part = jnp.dot(left[:, group * width:(group + 1) * width], right[group * width:(group + 1) * width], preferred_element_type=jnp.float32)
        total = total + lax.optimization_barrier(part.astype(jnp.bfloat16)).astype(jnp.float32)
    return total

def attend(projected, head_dim):
    tokens = projected.shape[0]
    parts = projected.astype(jnp.bfloat16).reshape(tokens, -1, 3, head_dim)
    queries = parts[:, :, 0, :]
    key_rows = parts[:, :, 1, :]
    value_rows = parts[:, :, 2, :]
    score_scale = 1.0 / math.sqrt(head_dim)
    scores = jnp.einsum('qhd,khd->hqk', queries.astype(jnp.float32), key_rows.astype(jnp.float32)) * score_scale
    later = lax.broadcasted_iota(jnp.int32, (tokens, tokens), 0)
    earlier = lax.broadcasted_iota(jnp.int32, (tokens, tokens), 1)
    exponent = jnp.where(earlier <= later, jnp.exp(scores), 0.0)
    probabilities = exponent / lax.optimization_barrier(jnp.sum(exponent, axis=-1, keepdims=True))
    attn_weights = probabilities.astype(jnp.bfloat16)
    attended = jnp.einsum('hqk,khd->qhd', attn_weights.astype(jnp.float32), value_rows.astype(jnp.float32)).astype(jnp.bfloat16)
    return (queries, key_rows, value_rows, probabilities, attn_weights, attended)

def attend_back(queries, key_rows, value_rows, probabilities, attn_weights, grad_attended, head_dim):
    tokens = queries.shape[0]
    score_scale = 1.0 / math.sqrt(head_dim)
    grad_values = jnp.einsum('hqk,qhd->khd', attn_weights.astype(jnp.float32), grad_attended.astype(jnp.float32)).astype(jnp.bfloat16)
    grad_probs = jnp.einsum('qhd,khd->hqk', grad_attended.astype(jnp.float32), value_rows.astype(jnp.float32))
    row_dot = lax.optimization_barrier(jnp.sum(probabilities * grad_probs, axis=-1, keepdims=True))
    grad_scores = (probabilities * (grad_probs - row_dot) * score_scale).astype(jnp.bfloat16)
    grad_queries = jnp.einsum('hqk,khd->qhd', grad_scores.astype(jnp.float32), key_rows.astype(jnp.float32)).astype(jnp.bfloat16)
    grad_keys = jnp.einsum('hqk,qhd->khd', grad_scores.astype(jnp.float32), queries.astype(jnp.float32)).astype(jnp.bfloat16)
    return jnp.stack([grad_queries, grad_keys, grad_values], axis=2).reshape(tokens, -1)

def layer_forward(inflow, weight_in, weight_out, scale_gain):
    standard, inv_scale = normalize(inflow)
    normed = (standard * scale_gain).astype(jnp.bfloat16)
    projected = jnp.dot(normed, weight_in, preferred_element_type=jnp.float32)
    attended = attend(projected, HEAD_DIM)[5].reshape(inflow.shape[0], -1)
    summed = group_sum(attended, weight_out)
    return (inflow.astype(jnp.float32) + summed).astype(jnp.bfloat16)

def layer_backward(stored, upstream, weight_in, weight_out, scale_gain):
    tokens = stored.shape[0]
    standard, inv_scale = normalize(stored)
    normed = (standard * scale_gain).astype(jnp.bfloat16)
    projected = jnp.dot(normed, weight_in, preferred_element_type=jnp.float32)
    queries, key_rows, value_rows, probabilities, attn_weights, attended = attend(projected, HEAD_DIM)
    grad_attended = jnp.dot(upstream, weight_out.T, preferred_element_type=jnp.float32).astype(jnp.bfloat16).reshape(tokens, -1, HEAD_DIM)
    grad_projected = attend_back(queries, key_rows, value_rows, probabilities, attn_weights, grad_attended, HEAD_DIM)
    grad_normed = group_sum(grad_projected, weight_in.T)
    grad_hat = grad_normed * scale_gain
    grad_local = inv_scale * (grad_hat - lax.optimization_barrier(jnp.mean(grad_hat, axis=-1, keepdims=True)) - standard * lax.optimization_barrier(jnp.mean(grad_hat * standard, axis=-1, keepdims=True)))
    return (upstream.astype(jnp.float32) + grad_local).astype(jnp.bfloat16)

def reference(entering, arriving, stashed, parked, evict, cotangent, arriving_grad, qkv_weight, out_weight, norm_gain):
    section_ids = jnp.arange(SECTIONS, dtype=jnp.int32)

    def forward_section(previous, params):
        index, weight_in, weight_out, scale_gain, arrived = params
        shifted = jnp.concatenate([arrived[None], previous[:-1]], axis=0)
        inflow = jnp.where(index == 0, entering, shifted)
        produced = jnp.stack([layer_forward(inflow[step], weight_in, weight_out, scale_gain) for step in range(TICKS)])
        return (produced, (produced, inflow))
    ignored, (section_outputs, inflows) = lax.scan(forward_section, jnp.zeros_like(entering), (section_ids, qkv_weight, out_weight, norm_gain, arriving))
    mirror_flags = evict[::-1][:, :, None, None] == 1
    new_parked = jnp.where(mirror_flags, inflows[::-1], jnp.zeros_like(inflows))
    held = jnp.where(evict[:, :, None, None] == 1, parked[::-1], stashed)

    def backward_section(later, params):
        index, weight_in, weight_out, scale_gain, arrived, stored = params
        shifted = jnp.concatenate([arrived[None], later[:-1]], axis=0)
        upstream = jnp.where(index == SECTIONS - 1, cotangent, shifted)
        passed_all = jnp.stack([layer_backward(stored[step], upstream[step], weight_in, weight_out, scale_gain) for step in range(TICKS)])
        return (passed_all, passed_all)
    ignored, input_grads = lax.scan(backward_section, jnp.zeros_like(cotangent), (section_ids, qkv_weight, out_weight, norm_gain, arriving_grad, held), reverse=True)
    return (section_outputs, input_grads, new_parked)
```

```python
import functools
import math

import jax
import jax.numpy as jnp
from jax import lax
from jax.experimental import pallas as pl
from jax.experimental.pallas import tpu as pltpu
from jax.sharding import PartitionSpec as P

MESH = pl.DeviceIdType.MESH
HD = 128
BF = jnp.bfloat16
F32 = jnp.float32

X0, U0, H0, H1, X1, U1 = range(6)
RF0, RB0, RF1, RB1 = range(4)


def dot(a, b):
    return lax.dot_general(a, b, (((1,), (0,)), ((), ())), preferred_element_type=F32)


def dot_nt(a, b):
    return lax.dot_general(a, b, (((1,), (1,)), ((), ())), preferred_element_type=F32)


def dot_tn(a, b):
    return lax.dot_general(a, b, (((0,), (0,)), ((), ())), preferred_element_type=F32)


def kernel(
    ent, arr, stash, park, flags, cot, agr, wq_h, wo_h, gain_h,
    out_f, out_b, out_p,
    wq, wo, gain, stv, prk, flv, ag, normed, proj, att, gab, gpb, wgs,
    pbuf, dbuf, zbuf, rrecv, drecv, zrecv, zown, sbuf, srecv, szbuf, szrecv, ostage, pstage,
    lsem, ag_s, agz_r, agy_r, rs_s, rsr_r, rsd_r, rsz_r, st_s, st_r, m_s, m_r, hop_s, hop_r, o_s,
):
    s, t = lax.axis_index("section"), lax.axis_index("tensor")
    sections = lax.axis_size("section")
    y, z = lax.rem(t, 4), lax.div(t, 4)
    yi = [y, lax.rem(y + 1, 4), lax.rem(y + 2, 4), lax.rem(y + 3, 4)]
    zi = [z, lax.rem(z + 1, 4), lax.rem(z + 2, 4), lax.rem(z + 3, 4)]
    nxt, prv = lax.rem(s + 1, sections), lax.rem(s + sections - 1, sections)
    mir = sections - 1 - s
    ydev = lambda j: (s, z * 4 + yi[j])
    zdev = lambda k: (s, zi[k] * 4 + y)
    feats = normed.shape[1]

    def chunk(yy, zz):
        return yy * 4 + zz

    def cols(yy, zz):
        return pl.ds(pl.multiple_of((zz * 4 + yy) * 256, 256), 256)

    own = chunk(y, z)
    my_cols = cols(y, z)

    def rcopy(src, dst, ss, rs, dev):
        return pltpu.make_async_remote_copy(
            src_ref=src, dst_ref=dst, send_sem=ss, recv_sem=rs, device_id=dev, device_id_type=MESH
        )

    @pl.when(s == 0)
    def _():
        pltpu.make_async_copy(ent.at[0], ag.at[X0, own], lsem.at[0]).start()

    @pl.when(s > 0)
    def _():
        pltpu.make_async_copy(arr.at[0], ag.at[X0, own], lsem.at[0]).start()

    @pl.when(s == sections - 1)
    def _():
        pltpu.make_async_copy(cot.at[0], ag.at[U0, own], lsem.at[1]).start()

    @pl.when(s < sections - 1)
    def _():
        pltpu.make_async_copy(agr.at[0], ag.at[U0, own], lsem.at[1]).start()

    load_stash = pltpu.make_async_copy(stash.at[0], stv, lsem.at[2])
    load_stash.start()
    load_flags = pltpu.make_async_copy(flags, flv, lsem.at[6])
    load_flags.start()
    load_gain = pltpu.make_async_copy(gain_h, gain, lsem.at[3])
    load_gain.start()
    load_wq = pltpu.make_async_copy(wq_h.at[0], wq, lsem.at[4])
    load_wq.start()
    load_wo = pltpu.make_async_copy(wo_h.at[0], wo, lsem.at[5])
    load_wo.start()

    barrier = pltpu.get_barrier_semaphore()
    peers = [ydev(1), ydev(2), ydev(3), zdev(1), zdev(2), zdev(3), (nxt, t), (prv, t), (mir, t)]
    for dev in peers:
        pl.semaphore_signal(barrier, inc=1, device_id=dev, device_id_type=MESH)
    pl.semaphore_wait(barrier, len(peers))

    def gz_copy(a, k):
        return rcopy(ag.at[a, own], ag.at[a, own], ag_s.at[a], agz_r.at[a, k - 1], zdev(k))

    def gz_wait(a, k):
        c = chunk(y, zi[(4 - k) % 4])
        rcopy(ag.at[a, c], ag.at[a, c], ag_s.at[a], agz_r.at[a, k - 1], zdev((4 - k) % 4)).wait_recv()

    def ag_z(a):
        for k in (1, 3, 2):
            gz_copy(a, k).start()

    def ag_y1(a, k):
        c = chunk(y, zi[(4 - k) % 4])
        if k:
            gz_wait(a, k)
        rcopy(ag.at[a, c], ag.at[a, c], ag_s.at[a], agy_r.at[a, 0, k], ydev(1)).start()
        rcopy(ag.at[a, c], ag.at[a, c], ag_s.at[a], agy_r.at[a, 1, k], ydev(3)).start()

    def ag_y2(a, k):
        zz = zi[(4 - k) % 4]
        c = chunk(yi[3], zz)
        rcopy(ag.at[a, c], ag.at[a, c], ag_s.at[a], agy_r.at[a, 0, k], ydev(3)).wait_recv()
        top = ag.at[a, c, pl.ds(0, 64)]
        rcopy(top, top, ag_s.at[a], agy_r.at[a, 2, k], ydev(1)).start()
        c = chunk(yi[1], zz)
        rcopy(ag.at[a, c], ag.at[a, c], ag_s.at[a], agy_r.at[a, 1, k], ydev(1)).wait_recv()
        low = ag.at[a, c, pl.ds(64, 64)]
        rcopy(low, low, ag_s.at[a], agy_r.at[a, 3, k], ydev(3)).start()

    def ag_fin(a):
        for k in (0, 1, 3, 2):
            c = chunk(yi[2], zi[(4 - k) % 4])
            top, low = ag.at[a, c, pl.ds(0, 64)], ag.at[a, c, pl.ds(64, 64)]
            rcopy(top, top, ag_s.at[a], agy_r.at[a, 2, k], ydev(3)).wait_recv()
            rcopy(low, low, ag_s.at[a], agy_r.at[a, 3, k], ydev(1)).wait_recv()

    def y1_rest(a):
        for k in (1, 3, 2):
            ag_y1(a, k)

    def y2_all(a):
        for k in (0, 1, 3, 2):
            ag_y2(a, k)

    def layer_norm(a):
        def add(c, acc):
            return acc + ag[a, c].astype(F32)

        acc = lax.fori_loop(0, 16, add, jnp.zeros((128, 256), F32))
        mean = jnp.sum(acc, axis=1, keepdims=True) * (1.0 / feats)

        def var(c, acc):
            d = ag[a, c].astype(F32) - mean
            return acc + d * d

        acc = lax.fori_loop(0, 16, var, jnp.zeros((128, 256), F32))
        inv = lax.rsqrt(jnp.sum(acc, axis=1, keepdims=True) * (1.0 / feats) + 1e-05)

        def put(c, carry):
            cc = cols(lax.div(c, 4), lax.rem(c, 4))
            normed[:, cc] = ((ag[a, c].astype(F32) - mean) * inv * gain[:, cc]).astype(BF)
            return carry

        lax.fori_loop(0, 16, put, 0)
        return mean, inv

    def qkv():
        def tile(n, carry):
            nn = pl.ds(pl.multiple_of(n * 256, 256), 256)
            proj[:, nn] = dot(normed[...], wq[:, nn])
            return carry

        lax.fori_loop(0, 3, tile, 0)

    scale = 1.0 / math.sqrt(HD)

    def attention():
        rows = lax.broadcasted_iota(jnp.int32, (128, 128), 0)
        lanes = lax.broadcasted_iota(jnp.int32, (128, 128), 1)
        out = []
        for h in range(2):
            q, k, v = (proj[:, h * 384 + i * 128 : h * 384 + (i + 1) * 128].astype(BF) for i in range(3))
            e = jnp.where(lanes <= rows, jnp.exp(dot_nt(q, k) * scale), 0.0)
            p = e / jnp.sum(e, axis=1, keepdims=True)
            out.append((q, k, v, p, p.astype(BF)))
        return out

    def attended(heads):
        for h, (q, k, v, p, w) in enumerate(heads):
            att[:, h * 128 : (h + 1) * 128] = dot(w, v).astype(BF)

    def grad_att(a):
        def step(c, acc):
            return acc + dot_nt(ag[a, c], wo[:, cols(lax.div(c, 4), lax.rem(c, 4))])

        gab[...] = lax.fori_loop(0, 16, step, jnp.zeros((128, 256), F32)).astype(BF)

    def attend_back(heads):
        for h, (q, k, v, p, w) in enumerate(heads):
            ga = gab[:, h * 128 : (h + 1) * 128]
            gv = dot_tn(w, ga).astype(BF)
            g = dot_nt(ga, v)
            gs = (p * (g - jnp.sum(p * g, axis=1, keepdims=True)) * scale).astype(BF)
            gpb[:, h * 384 : h * 384 + 128] = dot(gs, k).astype(BF)
            gpb[:, h * 384 + 128 : h * 384 + 256] = dot_tn(gs, q).astype(BF)
            gpb[:, h * 384 + 256 : h * 384 + 384] = gv

    def stats_start(tick):
        g = gpb[...].astype(F32)
        s1 = jnp.sum(g * wgs[...], axis=1, keepdims=True)
        s2 = jnp.sum(g * proj[...], axis=1, keepdims=True)
        lanes = lax.broadcasted_iota(jnp.int32, (128, 128), 1)
        both = jnp.where(lanes == 0, s1, jnp.where(lanes == 1, s2, 0.0))
        sbuf[tick] = both.T[0:8]
        for j in (1, 2, 3):
            rcopy(sbuf.at[tick], srecv.at[tick, j - 1], st_s.at[tick, j - 1], st_r.at[tick, j - 1], ydev(j)).start()

    def stats_mid(tick):
        for j in (1, 2, 3):
            rcopy(sbuf.at[tick], srecv.at[tick, j - 1], st_s.at[tick, j - 1], st_r.at[tick, j - 1], ydev(4 - j)).wait()
        szbuf[tick] = sbuf[tick] + srecv[tick, 0] + srecv[tick, 1] + srecv[tick, 2]
        for k in (1, 2, 3):
            rcopy(szbuf.at[tick], szrecv.at[tick, k - 1], st_s.at[tick, k + 2], st_r.at[tick, k + 2], zdev(k)).start()

    def stats_end(tick):
        for k in (1, 2, 3):
            rcopy(szbuf.at[tick], szrecv.at[tick, k - 1], st_s.at[tick, k + 2], st_r.at[tick, k + 2], zdev(4 - k)).wait()
        total = szbuf[tick] + szrecv[tick, 0] + szrecv[tick, 1] + szrecv[tick, 2]
        back = jnp.concatenate([total, jnp.zeros((120, 128), F32)], axis=0).T
        return back[:, 0:1] * (1.0 / feats), back[:, 1:2] * (1.0 / feats)

    KS = (1, 3, 2, 0)

    def part(r, yy, zz):
        if r in (RF0, RF1):
            return dot(att[...], wo[:, cols(yy, zz)])
        return dot_nt(gpb[...], wq[cols(yy, zz), :])

    def rs_o(r):
        for k in KS:
            pbuf[r, 2, k] = part(r, yi[2], zi[k]).astype(BF)
            top, low = pl.ds(0, 64), pl.ds(64, 64)
            rcopy(pbuf.at[r, 2, k, top], rrecv.at[r, k, top], rs_s.at[r], rsr_r.at[r, 0, k], ydev(1)).start()
            rcopy(pbuf.at[r, 2, k, low], rrecv.at[r, k, low], rs_s.at[r], rsr_r.at[r, 1, k], ydev(3)).start()
        for k in KS:
            pbuf[r, 1, k] = part(r, yi[1], zi[k]).astype(BF)
            pbuf[r, 3, k] = part(r, yi[3], zi[k]).astype(BF)
        for k in KS:
            pbuf[r, 0, k] = part(r, y, zi[k]).astype(BF)

    def rs_d(r):
        top, low = pl.ds(0, 64), pl.ds(64, 64)
        for k in KS:
            rcopy(pbuf.at[r, 2, k, top], rrecv.at[r, k, top], rs_s.at[r], rsr_r.at[r, 0, k], ydev(3)).wait_recv()
            dbuf[r, 0, k, 0:64] = (pbuf[r, 1, k, 0:64].astype(F32) + rrecv[r, k, 0:64].astype(F32)).astype(BF)
            dbuf[r, 0, k, 64:128] = pbuf[r, 1, k, 64:128]
            rcopy(dbuf.at[r, 0, k], drecv.at[r, 0, k], rs_s.at[r], rsd_r.at[r, 0, k], ydev(1)).start()
            rcopy(pbuf.at[r, 2, k, low], rrecv.at[r, k, low], rs_s.at[r], rsr_r.at[r, 1, k], ydev(1)).wait_recv()
            dbuf[r, 1, k, 0:64] = pbuf[r, 3, k, 0:64]
            dbuf[r, 1, k, 64:128] = (pbuf[r, 3, k, 64:128].astype(F32) + rrecv[r, k, 64:128].astype(F32)).astype(BF)
            rcopy(dbuf.at[r, 1, k], drecv.at[r, 1, k], rs_s.at[r], rsd_r.at[r, 1, k], ydev(3)).start()

    def rs_z(r):
        for k in KS:
            rcopy(dbuf.at[r, 0, k], drecv.at[r, 0, k], rs_s.at[r], rsd_r.at[r, 0, k], ydev(3)).wait_recv()
            rcopy(dbuf.at[r, 1, k], drecv.at[r, 1, k], rs_s.at[r], rsd_r.at[r, 1, k], ydev(1)).wait_recv()
            total = pbuf[r, 0, k].astype(F32) + drecv[r, 0, k].astype(F32) + drecv[r, 1, k].astype(F32)
            if k:
                zbuf[r, k - 1] = total.astype(BF)
                rcopy(zbuf.at[r, k - 1], zrecv.at[r, k - 1], rs_s.at[r], rsz_r.at[r, k - 1], zdev(k)).start()
            else:
                zown[r] = total

    def rs_fin(r):
        for k in (1, 3, 2):
            rcopy(zbuf.at[r, k - 1], zrecv.at[r, k - 1], rs_s.at[r], rsz_r.at[r, k - 1], zdev(4 - k)).wait_recv()
        return (
            zown[r] + zrecv[r, 0].astype(F32) + zrecv[r, 1].astype(F32) + zrecv[r, 2].astype(F32)
        )

    def forward_end(tick):
        total = rs_fin(RF1 if tick else RF0)
        ostage[tick] = (ag[X1 if tick else X0, own].astype(F32) + total).astype(BF)
        pltpu.make_async_copy(ostage.at[tick], out_f.at[0, tick], o_s.at[tick]).start()

    def backward_end(tick, mean, inv):
        total = rs_fin(RB1 if tick else RB0)
        m1, m2 = stats_end(tick)
        std = (ag[H1 if tick else H0, own].astype(F32) - mean) * inv
        grad = inv * (total * gain[:, my_cols] - m1 - std * m2)
        ostage[2 + tick] = (ag[U1 if tick else U0, own].astype(F32) + grad).astype(BF)
        pltpu.make_async_copy(ostage.at[2 + tick], out_b.at[0, tick], o_s.at[2 + tick]).start()

    def hop_start(slot, a, forward):
        cp = rcopy(ostage.at[slot], ag.at[a, own], hop_s.at[slot // 2], hop_r.at[slot // 2], (nxt if forward else prv, t))

        @pl.when((s < sections - 1) if forward else (s > 0))
        def _():
            cp.start()

    def hop_wait(slot, a, forward, first):
        cp = rcopy(ostage.at[slot], ag.at[a, own], hop_s.at[slot // 2], hop_r.at[slot // 2], (prv if forward else nxt, t))

        @pl.when((s > 0) if forward else (s < sections - 1))
        def _():
            cp.wait_recv()

        @pl.when((s == 0) if forward else (s == sections - 1))
        def _():
            own_copy = pltpu.make_async_copy(first, ag.at[a, own], lsem.at[slot // 2])
            own_copy.start()
            own_copy.wait()

    def mirror_copy(tick):
        return rcopy(park.at[0, tick], prk.at[tick], m_s.at[tick], m_r.at[tick], (mir, t))

    def parked_copy(tick):
        return rcopy(pstage.at[tick], out_p.at[0, tick], m_s.at[2 + tick], m_r.at[2 + tick], (mir, t))

    def park_inflow(tick):
        mine = ag[X1 if tick else X0, own]
        pstage[tick] = jnp.where(flv[tick] == 1, mine.astype(F32), 0.0).astype(BF)
        parked_copy(tick).start()

    def choose(tick):
        mirror_copy(tick).wait_recv()
        ag[H1 if tick else H0, own] = jnp.where(
            flv[tick] == 1, prk[tick].astype(F32), stv[tick].astype(F32)
        ).astype(BF)

    mirror_copy(0).start()
    pltpu.make_async_copy(arr.at[0], ag.at[X0, own], lsem.at[0]).wait()
    ag_z(X0)
    ag_y1(X0, 0)
    pltpu.make_async_copy(agr.at[0], ag.at[U0, own], lsem.at[1]).wait()
    mirror_copy(1).start()
    ag_z(U0)
    ag_y1(U0, 0)
    load_stash.wait()
    load_flags.wait()
    load_gain.wait()
    load_wq.wait()
    load_wo.wait()
    y1_rest(X0)
    y1_rest(U0)
    y2_all(X0)
    choose(0)
    ag_z(H0)
    ag_y1(H0, 0)
    g_hi = gain[...].astype(BF)
    g_lo = (gain[...] - g_hi.astype(F32)).astype(BF)
    sub = lax.broadcasted_iota(jnp.int32, (16, 128), 0)
    for c in range(feats // 128):
        hi, lo = g_hi[:, c * 128 : (c + 1) * 128].astype(F32), g_lo[:, c * 128 : (c + 1) * 128].astype(F32)
        normed[0:16, c * 128 : (c + 1) * 128] = jnp.where(sub == 0, hi, jnp.where(sub == 1, lo, 0.0)).astype(BF)

    def wg_tile(n, carry):
        nn = pl.ds(pl.multiple_of(n * 256, 256), 256)
        wgs[:, nn] = jnp.sum(dot(normed[0:16, :], wq[:, nn]), axis=0, keepdims=True)
        return carry

    lax.fori_loop(0, 3, wg_tile, 0)
    y2_all(U0)
    choose(1)
    y1_rest(H0)
    ag_fin(X0)
    layer_norm(X0)
    qkv()
    attended(attention())
    rs_o(RF0)
    y2_all(H0)
    ag_z(H1)
    rs_d(RF0)
    ag_fin(U0)
    grad_att(U0)
    park_inflow(0)
    rs_z(RF0)
    ag_fin(H0)
    mean0, inv0 = layer_norm(H0)
    qkv()
    heads = attention()
    attend_back(heads)
    stats_start(0)
    rs_o(RB0)
    forward_end(0)
    hop_start(0, X1, True)
    rs_d(RB0)
    ag_y1(H1, 0)
    y1_rest(H1)
    stats_mid(0)
    hop_wait(0, X1, True, ent.at[1])
    ag_z(X1)
    ag_y1(X1, 0)
    rs_z(RB0)
    y1_rest(X1)
    y2_all(H1)
    backward_end(0, mean0, inv0)
    hop_start(2, U1, False)
    y2_all(X1)
    ag_fin(H1)
    hop_wait(2, U1, False, cot.at[1])
    ag_z(U1)
    ag_y1(U1, 0)
    ag_fin(X1)
    layer_norm(X1)
    qkv()
    attended(attention())
    y1_rest(U1)
    rs_o(RF1)
    y2_all(U1)
    rs_d(RF1)
    mean1, inv1 = layer_norm(H1)
    qkv()
    heads = attention()
    park_inflow(1)
    rs_z(RF1)
    ag_fin(U1)
    grad_att(U1)
    attend_back(heads)
    stats_start(1)
    rs_o(RB1)
    rs_d(RB1)
    stats_mid(1)
    forward_end(1)
    rs_z(RB1)
    backward_end(1, mean1, inv1)

    for a in range(6):
        pltpu.make_async_copy(ag.at[a, pl.ds(0, 15)], ag.at[a, pl.ds(0, 15)], ag_s.at[a]).wait()
    for r in range(4):
        pltpu.make_async_copy(ag.at[0, pl.ds(0, 15)], ag.at[0, pl.ds(0, 15)], rs_s.at[r]).wait()
    for tick in range(2):
        mirror_copy(tick).wait_send()
        parked_copy(tick).wait()
        pltpu.make_async_copy(ostage.at[tick], out_f.at[0, tick], o_s.at[tick]).wait()
        pltpu.make_async_copy(ostage.at[2 + tick], out_b.at[0, tick], o_s.at[2 + tick]).wait()

    @pl.when(s < sections - 1)
    def _():
        rcopy(ostage.at[0], ag.at[X1, own], hop_s.at[0], hop_r.at[0], (nxt, t)).wait_send()

    @pl.when(s > 0)
    def _():
        rcopy(ostage.at[2], ag.at[U1, own], hop_s.at[1], hop_r.at[1], (prv, t)).wait_send()


def on_device(entering, arriving, stashed, parked, evict, cotangent, arriving_grad, qkv_weight, out_weight, norm_gain):
    any_spec = pl.BlockSpec(memory_space=pl.ANY)
    flags = jnp.broadcast_to(evict[0][:, None, None], (2, 128, 256))
    piece = lambda *lead: pltpu.VMEM(tuple(lead) + (128, 256), BF)
    dma = lambda *shape: pltpu.SemaphoreType.DMA(shape)
    slab = jax.ShapeDtypeStruct((1, 2, 128, 256), BF)
    return pl.pallas_call(
        kernel,
        out_shape=(slab, slab, slab),
        in_specs=[any_spec] * 10,
        out_specs=(any_spec,) * 3,
        scratch_shapes=[
            pltpu.VMEM(qkv_weight.shape[1:], BF),
            pltpu.VMEM(out_weight.shape[1:], BF),
            pltpu.VMEM(norm_gain.shape, F32),
            piece(2),
            piece(2),
            pltpu.VMEM((2, 128, 256), jnp.int32),
            piece(6, 16),
            pltpu.VMEM((128, 4096), BF),
            pltpu.VMEM((128, 768), F32),
            pltpu.VMEM((128, 256), BF),
            pltpu.VMEM((128, 256), BF),
            pltpu.VMEM((128, 768), BF),
            pltpu.VMEM((1, 768), F32),
            piece(4, 4, 4),
            piece(4, 2, 4),
            piece(4, 3),
            piece(4, 4),
            piece(4, 2, 4),
            piece(4, 3),
            pltpu.VMEM((4, 128, 256), F32),
            pltpu.VMEM((2, 8, 128), F32),
            pltpu.VMEM((2, 3, 8, 128), F32),
            pltpu.VMEM((2, 8, 128), F32),
            pltpu.VMEM((2, 3, 8, 128), F32),
            piece(4),
            piece(2),
            dma(7),
            dma(6),
            dma(6, 3),
            dma(6, 4, 4),
            dma(4),
            dma(4, 2, 4),
            dma(4, 2, 4),
            dma(4, 3),
            dma(2, 6),
            dma(2, 6),
            dma(4),
            dma(4),
            dma(2),
            dma(2),
            dma(4),
        ],
        compiler_params=pltpu.CompilerParams(
            collective_id=0, has_side_effects=True, vmem_limit_bytes=56 * 2**20
        ),
        cost_estimate=pl.CostEstimate(flops=6 * 10**9, bytes_accessed=10**7, transcendentals=10**5),
        name="relay_window",
    )(entering, arriving, stashed, parked, flags, cotangent, arriving_grad, qkv_weight, out_weight, norm_gain)


def solution(mesh):
    in_specs = (
        P(None, None, "tensor"),
        P("section", None, "tensor"),
        P("section", None, None, "tensor"),
        P("section", None, None, "tensor"),
        P("section", None),
        P(None, None, "tensor"),
        P("section", None, "tensor"),
        P("section", None, "tensor"),
        P("section", "tensor", None),
        P("section", None),
    )
    out_specs = (P("section", None, None, "tensor"),) * 3
    return jax.shard_map(on_device, mesh=mesh, in_specs=in_specs, out_specs=out_specs, check_vma=False)
```

```python
import functools
import math

import jax
import jax.numpy as jnp
from jax import lax
from jax.experimental import pallas as pl
from jax.experimental.pallas import tpu as pltpu
from jax.sharding import PartitionSpec as P

MESH = pl.DeviceIdType.MESH
HD = 128
BF = jnp.bfloat16
F32 = jnp.float32

X0, U0, H0, H1, X1, U1 = range(6)
RF0, RB0, RF1, RB1 = range(4)


def dot(a, b):
    return lax.dot_general(a, b, (((1,), (0,)), ((), ())), preferred_element_type=F32)


def dot_nt(a, b):
    return lax.dot_general(a, b, (((1,), (1,)), ((), ())), preferred_element_type=F32)


def dot_tn(a, b):
    return lax.dot_general(a, b, (((0,), (0,)), ((), ())), preferred_element_type=F32)


def kernel(
    ent, arr, stash, park, flags, cot, agr, wq_h, wo_h, gain_h,
    out_all,
    wq, wo, gain, p1, stv, prk, flv, ag, normed, proj, att, gab, gpb, wgs,
    pbuf, dbuf, zbuf, rrecv, drecv, zrecv, zown, sbuf, srecv, szbuf, szrecv, ostage, pstage,
    lsem, ag_s, agz_r, agy_r, rs_s, rsr_r, rsd_r, rsz_r, st_s, st_r, m_s, m_r, hop_s, hop_r, o_s,
):
    s, t = lax.axis_index("section"), lax.axis_index("tensor")
    sections = lax.axis_size("section")
    y, z = lax.rem(t, 4), lax.div(t, 4)
    yi = [y, lax.rem(y + 1, 4), lax.rem(y + 2, 4), lax.rem(y + 3, 4)]
    zi = [z, lax.rem(z + 1, 4), lax.rem(z + 2, 4), lax.rem(z + 3, 4)]
    nxt, prv = lax.rem(s + 1, sections), lax.rem(s + sections - 1, sections)
    mir = sections - 1 - s
    ydev = lambda j: (s, z * 4 + yi[j])
    zdev = lambda k: (s, zi[k] * 4 + y)
    feats = normed.shape[1]

    def chunk(yy, zz):
        return yy * 4 + zz

    def cols(yy, zz):
        return pl.ds(pl.multiple_of((zz * 4 + yy) * 256, 256), 256)

    own = chunk(y, z)
    my_cols = cols(y, z)

    def rcopy(src, dst, ss, rs, dev):
        return pltpu.make_async_remote_copy(
            src_ref=src, dst_ref=dst, send_sem=ss, recv_sem=rs, device_id=dev, device_id_type=MESH
        )

    @pl.when(s == 0)
    def _():
        pltpu.make_async_copy(ent.at[0], ag.at[X0, own], lsem.at[0]).start()

    @pl.when(s > 0)
    def _():
        pltpu.make_async_copy(arr.at[0], ag.at[X0, own], lsem.at[0]).start()

    @pl.when(s == sections - 1)
    def _():
        pltpu.make_async_copy(cot.at[0], ag.at[U0, own], lsem.at[1]).start()

    @pl.when(s < sections - 1)
    def _():
        pltpu.make_async_copy(agr.at[0], ag.at[U0, own], lsem.at[1]).start()

    load_stash = pltpu.make_async_copy(stash.at[0], stv, lsem.at[2])
    load_stash.start()
    load_flags = pltpu.make_async_copy(flags, flv, lsem.at[6])
    load_flags.start()
    load_gain = pltpu.make_async_copy(gain_h, gain, lsem.at[3])
    load_gain.start()
    load_wq = pltpu.make_async_copy(wq_h.at[0], wq, lsem.at[4])
    load_wq.start()
    load_wo = pltpu.make_async_copy(wo_h.at[0], wo, lsem.at[5])
    load_wo.start()

    barrier = pltpu.get_barrier_semaphore()
    peers = [ydev(1), ydev(2), ydev(3), zdev(1), zdev(2), zdev(3), (nxt, t), (prv, t), (mir, t)]
    for dev in peers:
        pl.semaphore_signal(barrier, inc=1, device_id=dev, device_id_type=MESH)
    pl.semaphore_wait(barrier, len(peers))

    def gz_copy(a, k):
        return rcopy(ag.at[a, own], ag.at[a, own], ag_s.at[a], agz_r.at[a, k - 1], zdev(k))

    def gz_wait(a, k):
        c = chunk(y, zi[(4 - k) % 4])
        rcopy(ag.at[a, c], ag.at[a, c], ag_s.at[a], agz_r.at[a, k - 1], zdev((4 - k) % 4)).wait_recv()

    def ag_z(a):
        for k in (1, 3, 2):
            gz_copy(a, k).start()

    def ag_y1(a, k):
        c = chunk(y, zi[(4 - k) % 4])
        if k:
            gz_wait(a, k)
        rcopy(ag.at[a, c], ag.at[a, c], ag_s.at[a], agy_r.at[a, 0, k], ydev(1)).start()
        rcopy(ag.at[a, c], ag.at[a, c], ag_s.at[a], agy_r.at[a, 1, k], ydev(3)).start()

    def ag_y2(a, k):
        zz = zi[(4 - k) % 4]
        c = chunk(yi[3], zz)
        rcopy(ag.at[a, c], ag.at[a, c], ag_s.at[a], agy_r.at[a, 0, k], ydev(3)).wait_recv()
        top = ag.at[a, c, pl.ds(0, 64)]
        rcopy(top, top, ag_s.at[a], agy_r.at[a, 2, k], ydev(1)).start()
        c = chunk(yi[1], zz)
        rcopy(ag.at[a, c], ag.at[a, c], ag_s.at[a], agy_r.at[a, 1, k], ydev(1)).wait_recv()
        low = ag.at[a, c, pl.ds(64, 64)]
        rcopy(low, low, ag_s.at[a], agy_r.at[a, 3, k], ydev(3)).start()

    def ag_fin(a):
        for k in (0, 1, 3, 2):
            c = chunk(yi[2], zi[(4 - k) % 4])
            top, low = ag.at[a, c, pl.ds(0, 64)], ag.at[a, c, pl.ds(64, 64)]
            rcopy(top, top, ag_s.at[a], agy_r.at[a, 2, k], ydev(3)).wait_recv()
            rcopy(low, low, ag_s.at[a], agy_r.at[a, 3, k], ydev(1)).wait_recv()

    def y1_rest(a):
        for k in (1, 3, 2):
            ag_y1(a, k)

    def y2_all(a):
        for k in (0, 1, 3, 2):
            ag_y2(a, k)

    def layer_norm(a):
        def add(c, acc):
            return acc + ag[a, c].astype(F32)

        acc = lax.fori_loop(0, 16, add, jnp.zeros((128, 256), F32))
        mean = jnp.sum(acc, axis=1, keepdims=True) * (1.0 / feats)

        def var(c, acc):
            d = ag[a, c].astype(F32) - mean
            return acc + d * d

        acc = lax.fori_loop(0, 16, var, jnp.zeros((128, 256), F32))
        inv = lax.rsqrt(jnp.sum(acc, axis=1, keepdims=True) * (1.0 / feats) + 1e-05)

        def put(c, carry):
            cc = cols(lax.div(c, 4), lax.rem(c, 4))
            normed[:, cc] = ((ag[a, c].astype(F32) - mean) * inv * gain[:, cc]).astype(BF)
            return carry

        lax.fori_loop(0, 16, put, 0)
        return mean, inv

    def qkv():
        def tile(n, carry):
            nn = pl.ds(pl.multiple_of(n * 256, 256), 256)
            proj[:, nn] = dot(normed[...], wq[:, nn])
            return carry

        lax.fori_loop(0, 3, tile, 0)

    scale = 1.0 / math.sqrt(HD)

    def attention():
        rows = lax.broadcasted_iota(jnp.int32, (128, 128), 0)
        lanes = lax.broadcasted_iota(jnp.int32, (128, 128), 1)
        out = []
        for h in range(2):
            q, k, v = (proj[:, h * 384 + i * 128 : h * 384 + (i + 1) * 128].astype(BF) for i in range(3))
            e = jnp.where(lanes <= rows, jnp.exp(dot_nt(q, k) * scale), 0.0)
            p = e / jnp.sum(e, axis=1, keepdims=True)
            out.append((q, k, v, p, p.astype(BF)))
        return out

    def attended(heads):
        for h, (q, k, v, p, w) in enumerate(heads):
            att[:, h * 128 : (h + 1) * 128] = dot(w, v).astype(BF)

    def grad_att(a):
        def step(c, acc):
            return acc + dot_nt(ag[a, c], wo[:, cols(lax.div(c, 4), lax.rem(c, 4))])

        gab[...] = lax.fori_loop(0, 16, step, jnp.zeros((128, 256), F32)).astype(BF)

    def attend_back(heads):
        for h, (q, k, v, p, w) in enumerate(heads):
            ga = gab[:, h * 128 : (h + 1) * 128]
            gv = dot_tn(w, ga).astype(BF)
            g = dot_nt(ga, v)
            gs = (p * (g - jnp.sum(p * g, axis=1, keepdims=True)) * scale).astype(BF)
            gpb[:, h * 384 : h * 384 + 128] = dot(gs, k).astype(BF)
            gpb[:, h * 384 + 128 : h * 384 + 256] = dot_tn(gs, q).astype(BF)
            gpb[:, h * 384 + 256 : h * 384 + 384] = gv

    def stats_start(tick):
        g = gpb[...].astype(F32)
        s1 = jnp.sum(g * wgs[...], axis=1, keepdims=True)
        s2 = jnp.sum(g * proj[...], axis=1, keepdims=True)
        lanes = lax.broadcasted_iota(jnp.int32, (128, 128), 1)
        both = jnp.where(lanes == 0, s1, jnp.where(lanes == 1, s2, 0.0))
        sbuf[tick] = both.T[0:8]
        for j in (1, 2, 3):
            rcopy(sbuf.at[tick], srecv.at[tick, j - 1], st_s.at[tick, j - 1], st_r.at[tick, j - 1], ydev(j)).start()

    def stats_mid(tick):
        for j in (1, 2, 3):
            rcopy(sbuf.at[tick], srecv.at[tick, j - 1], st_s.at[tick, j - 1], st_r.at[tick, j - 1], ydev(4 - j)).wait()
        szbuf[tick] = sbuf[tick] + srecv[tick, 0] + srecv[tick, 1] + srecv[tick, 2]
        for k in (1, 2, 3):
            rcopy(szbuf.at[tick], szrecv.at[tick, k - 1], st_s.at[tick, k + 2], st_r.at[tick, k + 2], zdev(k)).start()

    def stats_end(tick):
        for k in (1, 2, 3):
            rcopy(szbuf.at[tick], szrecv.at[tick, k - 1], st_s.at[tick, k + 2], st_r.at[tick, k + 2], zdev(4 - k)).wait()
        total = szbuf[tick] + szrecv[tick, 0] + szrecv[tick, 1] + szrecv[tick, 2]
        back = jnp.concatenate([total, jnp.zeros((120, 128), F32)], axis=0).T
        return back[:, 0:1] * (1.0 / feats), back[:, 1:2] * (1.0 / feats)

    KS = (1, 3, 2, 0)

    def part(r, yy, zz):
        if r in (RF0, RF1):
            return dot(att[...], wo[:, cols(yy, zz)])
        return dot_nt(gpb[...], wq[cols(yy, zz), :])

    def rs_o(r):
        for k in KS:
            pbuf[r, 2, k] = part(r, yi[2], zi[k]).astype(BF)
            top, low = pl.ds(0, 64), pl.ds(64, 64)
            rcopy(pbuf.at[r, 2, k, top], rrecv.at[r, k, top], rs_s.at[r], rsr_r.at[r, 0, k], ydev(1)).start()
            rcopy(pbuf.at[r, 2, k, low], rrecv.at[r, k, low], rs_s.at[r], rsr_r.at[r, 1, k], ydev(3)).start()
        for k in KS:
            pbuf[r, 1, k] = part(r, yi[1], zi[k]).astype(BF)
            pbuf[r, 3, k] = part(r, yi[3], zi[k]).astype(BF)
        for k in KS:
            pbuf[r, 0, k] = part(r, y, zi[k]).astype(BF)

    def rs_d(r):
        top, low = pl.ds(0, 64), pl.ds(64, 64)
        for k in KS:
            rcopy(pbuf.at[r, 2, k, top], rrecv.at[r, k, top], rs_s.at[r], rsr_r.at[r, 0, k], ydev(3)).wait_recv()
            dbuf[r, 0, k, 0:64] = (pbuf[r, 1, k, 0:64].astype(F32) + rrecv[r, k, 0:64].astype(F32)).astype(BF)
            dbuf[r, 0, k, 64:128] = pbuf[r, 1, k, 64:128]
            rcopy(dbuf.at[r, 0, k], drecv.at[r, 0, k], rs_s.at[r], rsd_r.at[r, 0, k], ydev(1)).start()
            rcopy(pbuf.at[r, 2, k, low], rrecv.at[r, k, low], rs_s.at[r], rsr_r.at[r, 1, k], ydev(1)).wait_recv()
            dbuf[r, 1, k, 0:64] = pbuf[r, 3, k, 0:64]
            dbuf[r, 1, k, 64:128] = (pbuf[r, 3, k, 64:128].astype(F32) + rrecv[r, k, 64:128].astype(F32)).astype(BF)
            rcopy(dbuf.at[r, 1, k], drecv.at[r, 1, k], rs_s.at[r], rsd_r.at[r, 1, k], ydev(3)).start()

    def rs_z(r):
        for k in KS:
            rcopy(dbuf.at[r, 0, k], drecv.at[r, 0, k], rs_s.at[r], rsd_r.at[r, 0, k], ydev(3)).wait_recv()
            rcopy(dbuf.at[r, 1, k], drecv.at[r, 1, k], rs_s.at[r], rsd_r.at[r, 1, k], ydev(1)).wait_recv()
            total = pbuf[r, 0, k].astype(F32) + drecv[r, 0, k].astype(F32) + drecv[r, 1, k].astype(F32)
            if k:
                zbuf[r, k - 1] = total.astype(BF)
                rcopy(zbuf.at[r, k - 1], zrecv.at[r, k - 1], rs_s.at[r], rsz_r.at[r, k - 1], zdev(k)).start()
            else:
                zown[r] = total

    def rs_fin(r):
        for k in (1, 3, 2):
            rcopy(zbuf.at[r, k - 1], zrecv.at[r, k - 1], rs_s.at[r], rsz_r.at[r, k - 1], zdev(4 - k)).wait_recv()
        return (
            zown[r] + zrecv[r, 0].astype(F32) + zrecv[r, 1].astype(F32) + zrecv[r, 2].astype(F32)
        )

    def forward_end(tick):
        total = rs_fin(RF1 if tick else RF0)
        ostage[tick] = (ag[X1 if tick else X0, own].astype(F32) + total).astype(BF)
        pltpu.make_async_copy(ostage.at[tick], out_all.at[0, tick], o_s.at[tick]).start()

    def backward_end(tick, mean, inv):
        total = rs_fin(RB1 if tick else RB0)
        m1, m2 = stats_end(tick)
        std = (ag[H1 if tick else H0, own].astype(F32) - mean) * inv
        grad = inv * (total * gain[:, my_cols] - m1 - std * m2)
        ostage[2 + tick] = (ag[U1 if tick else U0, own].astype(F32) + grad).astype(BF)
        pltpu.make_async_copy(ostage.at[2 + tick], out_all.at[1, tick], o_s.at[2 + tick]).start()

    def hop_start(slot, a, forward):
        cp = rcopy(ostage.at[slot], ag.at[a, own], hop_s.at[slot // 2], hop_r.at[slot // 2], (nxt if forward else prv, t))

        @pl.when((s < sections - 1) if forward else (s > 0))
        def _():
            cp.start()

    def hop_wait(slot, a, forward, first):
        cp = rcopy(ostage.at[slot], ag.at[a, own], hop_s.at[slot // 2], hop_r.at[slot // 2], (prv if forward else nxt, t))

        @pl.when((s > 0) if forward else (s < sections - 1))
        def _():
            cp.wait_recv()

        @pl.when((s == 0) if forward else (s == sections - 1))
        def _():
            own_copy = pltpu.make_async_copy(first, ag.at[a, own], lsem.at[slot // 2])
            own_copy.start()
            own_copy.wait()

    def mirror_copy(tick):
        return rcopy(park.at[0, tick], prk.at[tick], m_s.at[tick], m_r.at[tick], (mir, t))

    def parked_copy(tick):
        return rcopy(pstage.at[tick], out_all.at[2, tick], m_s.at[2 + tick], m_r.at[2 + tick], (mir, t))

    def park_inflow(tick):
        mine = ag[X1 if tick else X0, own]
        pstage[tick] = jnp.where(flv[:, tick : tick + 1] == 1, mine.astype(F32), 0.0).astype(BF)
        parked_copy(tick).start()

    def choose(tick):
        mirror_copy(tick).wait_recv()
        ag[H1 if tick else H0, own] = jnp.where(
            flv[:, tick : tick + 1] == 1, prk[tick].astype(F32), stv[tick].astype(F32)
        ).astype(BF)

    mirror_copy(0).start()
    pltpu.make_async_copy(arr.at[0], ag.at[X0, own], lsem.at[0]).wait()
    ag_z(X0)
    ag_y1(X0, 0)
    pltpu.make_async_copy(agr.at[0], ag.at[U0, own], lsem.at[1]).wait()
    ag_z(U0)
    ag_y1(U0, 0)
    load_stash.wait()
    load_flags.wait()
    load_gain.wait()
    y1_rest(X0)
    choose(0)
    ag_z(H0)
    ag_y1(H0, 0)
    mirror_copy(1).start()
    y1_rest(U0)
    load_wq.wait()
    load_wo.wait()
    g_hi = gain[...].astype(BF)
    g_lo = (gain[...] - g_hi.astype(F32)).astype(BF)
    sub = lax.broadcasted_iota(jnp.int32, (16, 128), 0)
    for c in range(feats // 128):
        hi, lo = g_hi[:, c * 128 : (c + 1) * 128].astype(F32), g_lo[:, c * 128 : (c + 1) * 128].astype(F32)
        normed[0:16, c * 128 : (c + 1) * 128] = jnp.where(sub == 0, hi, jnp.where(sub == 1, lo, 0.0)).astype(BF)

    def wg_tile(n, carry):
        nn = pl.ds(pl.multiple_of(n * 256, 256), 256)
        wgs[:, nn] = jnp.sum(dot(normed[0:16, :], wq[:, nn]), axis=0, keepdims=True)
        return carry

    lax.fori_loop(0, 3, wg_tile, 0)
    y2_all(X0)
    y1_rest(H0)
    y2_all(U0)
    choose(1)
    ag_fin(X0)
    layer_norm(X0)
    qkv()
    attended(attention())
    y2_all(H0)
    rs_o(RF0)
    ag_fin(U0)
    grad_att(U0)
    rs_d(RF0)
    ag_fin(H0)
    mean0, inv0 = layer_norm(H0)
    rs_z(RF0)
    qkv()
    heads = attention()
    attend_back(heads)
    stats_start(0)
    rs_o(RB0)
    forward_end(0)
    hop_start(0, X1, True)
    ag_z(H1)
    stats_mid(0)
    rs_d(RB0)
    ag_y1(H1, 0)
    hop_wait(0, X1, True, ent.at[1])
    ag_z(X1)
    ag_y1(X1, 0)
    y1_rest(H1)
    rs_z(RB0)
    y1_rest(X1)
    y2_all(H1)
    backward_end(0, mean0, inv0)
    hop_start(2, U1, False)
    y2_all(X1)
    park_inflow(0)
    ag_fin(H1)
    mean1, inv1 = layer_norm(H1)
    hop_wait(2, U1, False, cot.at[1])
    ag_z(U1)
    ag_y1(U1, 0)
    qkv()
    heads = attention()
    p1[...] = proj[...]
    y1_rest(U1)
    ag_fin(X1)
    layer_norm(X1)
    y2_all(U1)
    qkv()
    attended(attention())
    rs_o(RF1)
    park_inflow(1)
    ag_fin(U1)
    grad_att(U1)
    attend_back(heads)
    proj[...] = p1[...]
    stats_start(1)
    rs_o(RB1)
    rs_d(RB1)
    rs_d(RF1)
    stats_mid(1)
    rs_z(RB1)
    rs_z(RF1)
    backward_end(1, mean1, inv1)
    forward_end(1)

    for a in range(6):
        pltpu.make_async_copy(ag.at[a, pl.ds(0, 15)], ag.at[a, pl.ds(0, 15)], ag_s.at[a]).wait()
    for r in range(4):
        pltpu.make_async_copy(ag.at[0, pl.ds(0, 15)], ag.at[0, pl.ds(0, 15)], rs_s.at[r]).wait()
    for tick in range(2):
        mirror_copy(tick).wait_send()
        parked_copy(tick).wait()
        pltpu.make_async_copy(ostage.at[tick], out_all.at[0, tick], o_s.at[tick]).wait()
        pltpu.make_async_copy(ostage.at[2 + tick], out_all.at[1, tick], o_s.at[2 + tick]).wait()

    @pl.when(s < sections - 1)
    def _():
        rcopy(ostage.at[0], ag.at[X1, own], hop_s.at[0], hop_r.at[0], (nxt, t)).wait_send()

    @pl.when(s > 0)
    def _():
        rcopy(ostage.at[2], ag.at[U1, own], hop_s.at[1], hop_r.at[1], (prv, t)).wait_send()


def on_device(entering, arriving, stashed, parked, evict, cotangent, arriving_grad, qkv_weight, out_weight, norm_gain):
    any_spec = pl.BlockSpec(memory_space=pl.ANY)
    piece = lambda *lead: pltpu.VMEM(tuple(lead) + (128, 256), BF)
    dma = lambda *shape: pltpu.SemaphoreType.DMA(shape)
    slab = jax.ShapeDtypeStruct((3, 2, 128, 256), BF)
    made = pl.pallas_call(
        kernel,
        out_shape=slab,
        in_specs=[any_spec] * 10,
        out_specs=any_spec,
        scratch_shapes=[
            pltpu.VMEM(qkv_weight.shape[1:], BF),
            pltpu.VMEM(out_weight.shape[1:], BF),
            pltpu.VMEM(norm_gain.shape, F32),
            pltpu.VMEM((128, 768), F32),
            piece(2),
            piece(2),
            pltpu.VMEM((1, 2), jnp.int32),
            piece(6, 16),
            pltpu.VMEM((128, 4096), BF),
            pltpu.VMEM((128, 768), F32),
            pltpu.VMEM((128, 256), BF),
            pltpu.VMEM((128, 256), BF),
            pltpu.VMEM((128, 768), BF),
            pltpu.VMEM((1, 768), F32),
            piece(4, 4, 4),
            piece(4, 2, 4),
            piece(4, 3),
            piece(4, 4),
            piece(4, 2, 4),
            piece(4, 3),
            pltpu.VMEM((4, 128, 256), F32),
            pltpu.VMEM((2, 8, 128), F32),
            pltpu.VMEM((2, 3, 8, 128), F32),
            pltpu.VMEM((2, 8, 128), F32),
            pltpu.VMEM((2, 3, 8, 128), F32),
            piece(4),
            piece(2),
            dma(7),
            dma(6),
            dma(6, 3),
            dma(6, 4, 4),
            dma(4),
            dma(4, 2, 4),
            dma(4, 2, 4),
            dma(4, 3),
            dma(2, 6),
            dma(2, 6),
            dma(4),
            dma(4),
            dma(2),
            dma(2),
            dma(4),
        ],
        compiler_params=pltpu.CompilerParams(
            collective_id=0, has_side_effects=True, vmem_limit_bytes=56 * 2**20
        ),
        cost_estimate=pl.CostEstimate(flops=6 * 10**9, bytes_accessed=10**7, transcendentals=10**5),
        name="relay_window",
    )(entering, arriving, stashed, parked, evict, cotangent, arriving_grad, qkv_weight, out_weight, norm_gain)

    return made[0:1], made[1:2], made[2:3]


def solution(mesh):
    in_specs = (
        P(None, None, "tensor"),
        P("section", None, "tensor"),
        P("section", None, None, "tensor"),
        P("section", None, None, "tensor"),
        P("section", None),
        P(None, None, "tensor"),
        P("section", None, "tensor"),
        P("section", None, "tensor"),
        P("section", "tensor", None),
        P("section", None),
    )
    out_specs = (P("section", None, None, "tensor"),) * 3
    return jax.shard_map(on_device, mesh=mesh, in_specs=in_specs, out_specs=out_specs, check_vma=False)
```

```python
import functools
import math

import jax
import jax.numpy as jnp
from jax import lax
from jax.experimental import pallas as pl
from jax.experimental.pallas import tpu as pltpu
from jax.sharding import PartitionSpec as P

MESH = pl.DeviceIdType.MESH
HD = 128
BF = jnp.bfloat16
F32 = jnp.float32

X0, U0, H0, H1, X1, U1 = range(6)
RF0, RB0, RF1, RB1 = range(4)


def dot(a, b):
    return lax.dot_general(a, b, (((1,), (0,)), ((), ())), preferred_element_type=F32)


def dot_nt(a, b):
    return lax.dot_general(a, b, (((1,), (1,)), ((), ())), preferred_element_type=F32)


def dot_tn(a, b):
    return lax.dot_general(a, b, (((0,), (0,)), ((), ())), preferred_element_type=F32)


def kernel(
    ent, arr, stash, park, flags, cot, agr, wq_h, wo_h, gain_h,
    out_all,
    wq, wo, gain, p1, gaf, stv, prk, flv, ag, normed, proj, att, gab, gpb, wgs,
    pbuf, dbuf, zbuf, rrecv, drecv, zrecv, zown, sbuf, srecv, szbuf, szrecv, ostage, pstage,
    lsem, ag_s, agz_r, agy_r, rs_s, rsr_r, rsd_r, rsz_r, st_s, st_r, m_s, m_r, hop_s, hop_r, fz_s, o_s,
):
    s, t = lax.axis_index("section"), lax.axis_index("tensor")
    sections = lax.axis_size("section")
    y, z = lax.rem(t, 4), lax.div(t, 4)
    yi = [y, lax.rem(y + 1, 4), lax.rem(y + 2, 4), lax.rem(y + 3, 4)]
    zi = [z, lax.rem(z + 1, 4), lax.rem(z + 2, 4), lax.rem(z + 3, 4)]
    nxt, prv = lax.rem(s + 1, sections), lax.rem(s + sections - 1, sections)
    mir = sections - 1 - s
    ydev = lambda j: (s, z * 4 + yi[j])
    zdev = lambda k: (s, zi[k] * 4 + y)
    feats = normed.shape[1]

    def chunk(yy, zz):
        return yy * 4 + zz

    def cols(yy, zz):
        return pl.ds(pl.multiple_of((zz * 4 + yy) * 256, 256), 256)

    own = chunk(y, z)
    my_cols = cols(y, z)

    def rcopy(src, dst, ss, rs, dev):
        return pltpu.make_async_remote_copy(
            src_ref=src, dst_ref=dst, send_sem=ss, recv_sem=rs, device_id=dev, device_id_type=MESH
        )

    @pl.when(s == 0)
    def _():
        pltpu.make_async_copy(ent.at[0], ag.at[X0, own], lsem.at[0]).start()

    @pl.when(s > 0)
    def _():
        pltpu.make_async_copy(arr.at[0], ag.at[X0, own], lsem.at[0]).start()

    @pl.when(s == sections - 1)
    def _():
        pltpu.make_async_copy(cot.at[0], ag.at[U0, own], lsem.at[1]).start()

    @pl.when(s < sections - 1)
    def _():
        pltpu.make_async_copy(agr.at[0], ag.at[U0, own], lsem.at[1]).start()

    load_stash = pltpu.make_async_copy(stash.at[0], stv, lsem.at[2])
    load_stash.start()
    load_flags = pltpu.make_async_copy(flags, flv, lsem.at[6])
    load_flags.start()
    load_gain = pltpu.make_async_copy(gain_h, gain, lsem.at[3])
    load_gain.start()
    load_wq = pltpu.make_async_copy(wq_h.at[0], wq, lsem.at[4])
    load_wq.start()
    load_wo = pltpu.make_async_copy(wo_h.at[0], wo, lsem.at[5])
    load_wo.start()

    barrier = pltpu.get_barrier_semaphore()
    peers = [ydev(1), ydev(2), ydev(3), zdev(1), zdev(2), zdev(3), (mir, t)]
    peers += [(sec, zi[k] * 4 + y) for sec in (nxt, prv) for k in range(4)]
    for dev in peers:
        pl.semaphore_signal(barrier, inc=1, device_id=dev, device_id_type=MESH)
    pl.semaphore_wait(barrier, len(peers))

    def gz_copy(a, k):
        return rcopy(ag.at[a, own], ag.at[a, own], ag_s.at[a], agz_r.at[a, k - 1], zdev(k))

    def gz_wait(a, k):
        c = chunk(y, zi[(4 - k) % 4])
        rcopy(ag.at[a, c], ag.at[a, c], ag_s.at[a], agz_r.at[a, k - 1], zdev((4 - k) % 4)).wait_recv()

    def ag_z(a):
        for k in (1, 3, 2):
            gz_copy(a, k).start()

    def ag_y1(a, k):
        c = chunk(y, zi[(4 - k) % 4])
        if k:
            gz_wait(a, k)
        rcopy(ag.at[a, c], ag.at[a, c], ag_s.at[a], agy_r.at[a, 0, k], ydev(1)).start()
        rcopy(ag.at[a, c], ag.at[a, c], ag_s.at[a], agy_r.at[a, 1, k], ydev(3)).start()

    def ag_y2(a, k):
        zz = zi[(4 - k) % 4]
        c = chunk(yi[3], zz)
        rcopy(ag.at[a, c], ag.at[a, c], ag_s.at[a], agy_r.at[a, 0, k], ydev(3)).wait_recv()
        top = ag.at[a, c, pl.ds(0, 64)]
        rcopy(top, top, ag_s.at[a], agy_r.at[a, 2, k], ydev(1)).start()
        c = chunk(yi[1], zz)
        rcopy(ag.at[a, c], ag.at[a, c], ag_s.at[a], agy_r.at[a, 1, k], ydev(1)).wait_recv()
        low = ag.at[a, c, pl.ds(64, 64)]
        rcopy(low, low, ag_s.at[a], agy_r.at[a, 3, k], ydev(3)).start()

    def ag_fin(a):
        for k in (0, 1, 3, 2):
            c = chunk(yi[2], zi[(4 - k) % 4])
            top, low = ag.at[a, c, pl.ds(0, 64)], ag.at[a, c, pl.ds(64, 64)]
            rcopy(top, top, ag_s.at[a], agy_r.at[a, 2, k], ydev(3)).wait_recv()
            rcopy(low, low, ag_s.at[a], agy_r.at[a, 3, k], ydev(1)).wait_recv()

    def y1_rest(a):
        for k in (1, 3, 2):
            ag_y1(a, k)

    def y2_all(a):
        for k in (0, 1, 3, 2):
            ag_y2(a, k)

    def layer_norm(a):
        def add(c, acc):
            return acc + ag[a, c].astype(F32)

        acc = lax.fori_loop(0, 16, add, jnp.zeros((128, 256), F32))
        mean = jnp.sum(acc, axis=1, keepdims=True) * (1.0 / feats)

        def var(c, acc):
            d = ag[a, c].astype(F32) - mean
            return acc + d * d

        acc = lax.fori_loop(0, 16, var, jnp.zeros((128, 256), F32))
        inv = lax.rsqrt(jnp.sum(acc, axis=1, keepdims=True) * (1.0 / feats) + 1e-05)

        def put(c, carry):
            cc = cols(lax.div(c, 4), lax.rem(c, 4))
            normed[:, cc] = ((ag[a, c].astype(F32) - mean) * inv * gain[:, cc]).astype(BF)
            return carry

        lax.fori_loop(0, 16, put, 0)
        return mean, inv

    def qkv():
        def tile(n, carry):
            nn = pl.ds(pl.multiple_of(n * 256, 256), 256)
            proj[:, nn] = dot(normed[...], wq[:, nn])
            return carry

        lax.fori_loop(0, 3, tile, 0)

    scale = 1.0 / math.sqrt(HD)

    def attention():
        rows = lax.broadcasted_iota(jnp.int32, (128, 128), 0)
        lanes = lax.broadcasted_iota(jnp.int32, (128, 128), 1)
        out = []
        for h in range(2):
            q, k, v = (proj[:, h * 384 + i * 128 : h * 384 + (i + 1) * 128].astype(BF) for i in range(3))
            e = jnp.where(lanes <= rows, jnp.exp(dot_nt(q, k) * scale), 0.0)
            p = e / jnp.sum(e, axis=1, keepdims=True)
            out.append((q, k, v, p, p.astype(BF)))
        return out

    def attended(heads):
        for h, (q, k, v, p, w) in enumerate(heads):
            att[:, h * 128 : (h + 1) * 128] = dot(w, v).astype(BF)

    def grad_cols(a, js, first):
        acc = first
        for j in js:

            def step(zz, acc, j=j):
                return acc + dot_nt(ag[a, chunk(yi[j], zz)], wo[:, cols(yi[j], zz)])

            acc = lax.fori_loop(0, 4, step, acc)
        return acc

    def grad_att3(a):
        gaf[...] = grad_cols(a, (0, 1, 3), jnp.zeros((128, 256), F32))

    def grad_att1(a):
        gab[...] = grad_cols(a, (2,), gaf[...]).astype(BF)

    def attend_back(heads):
        for h, (q, k, v, p, w) in enumerate(heads):
            ga = gab[:, h * 128 : (h + 1) * 128]
            gv = dot_tn(w, ga).astype(BF)
            g = dot_nt(ga, v)
            gs = (p * (g - jnp.sum(p * g, axis=1, keepdims=True)) * scale).astype(BF)
            gpb[:, h * 384 : h * 384 + 128] = dot(gs, k).astype(BF)
            gpb[:, h * 384 + 128 : h * 384 + 256] = dot_tn(gs, q).astype(BF)
            gpb[:, h * 384 + 256 : h * 384 + 384] = gv

    def stats_start(tick):
        g = gpb[...].astype(F32)
        s1 = jnp.sum(g * wgs[...], axis=1, keepdims=True)
        s2 = jnp.sum(g * proj[...], axis=1, keepdims=True)
        lanes = lax.broadcasted_iota(jnp.int32, (128, 128), 1)
        both = jnp.where(lanes == 0, s1, jnp.where(lanes == 1, s2, 0.0))
        sbuf[tick] = both.T[0:8]
        for j in (1, 2, 3):
            rcopy(sbuf.at[tick], srecv.at[tick, j - 1], st_s.at[tick, j - 1], st_r.at[tick, j - 1], ydev(j)).start()

    def stats_mid(tick):
        for j in (1, 2, 3):
            rcopy(sbuf.at[tick], srecv.at[tick, j - 1], st_s.at[tick, j - 1], st_r.at[tick, j - 1], ydev(4 - j)).wait()
        szbuf[tick] = sbuf[tick] + srecv[tick, 0] + srecv[tick, 1] + srecv[tick, 2]
        for k in (1, 2, 3):
            rcopy(szbuf.at[tick], szrecv.at[tick, k - 1], st_s.at[tick, k + 2], st_r.at[tick, k + 2], zdev(k)).start()

    def stats_end(tick):
        for k in (1, 2, 3):
            rcopy(szbuf.at[tick], szrecv.at[tick, k - 1], st_s.at[tick, k + 2], st_r.at[tick, k + 2], zdev(4 - k)).wait()
        total = szbuf[tick] + szrecv[tick, 0] + szrecv[tick, 1] + szrecv[tick, 2]
        back = jnp.concatenate([total, jnp.zeros((120, 128), F32)], axis=0).T
        return back[:, 0:1] * (1.0 / feats), back[:, 1:2] * (1.0 / feats)

    KS = (1, 3, 2, 0)

    def part(r, yy, zz):
        if r in (RF0, RF1):
            return dot(att[...], wo[:, cols(yy, zz)])
        return dot_nt(gpb[...], wq[cols(yy, zz), :])

    def rs_o(r):
        for k in KS:
            pbuf[r, 2, k] = part(r, yi[2], zi[k]).astype(BF)
            top, low = pl.ds(0, 64), pl.ds(64, 64)
            rcopy(pbuf.at[r, 2, k, top], rrecv.at[r, k, top], rs_s.at[r], rsr_r.at[r, 0, k], ydev(1)).start()
            rcopy(pbuf.at[r, 2, k, low], rrecv.at[r, k, low], rs_s.at[r], rsr_r.at[r, 1, k], ydev(3)).start()
        for k in KS:
            pbuf[r, 1, k] = part(r, yi[1], zi[k]).astype(BF)
            pbuf[r, 3, k] = part(r, yi[3], zi[k]).astype(BF)

    def rs_d(r):
        top, low = pl.ds(0, 64), pl.ds(64, 64)
        for k in KS:
            rcopy(pbuf.at[r, 2, k, top], rrecv.at[r, k, top], rs_s.at[r], rsr_r.at[r, 0, k], ydev(3)).wait_recv()
            dbuf[r, 0, k, 0:64] = (pbuf[r, 1, k, 0:64].astype(F32) + rrecv[r, k, 0:64].astype(F32)).astype(BF)
            dbuf[r, 0, k, 64:128] = pbuf[r, 1, k, 64:128]
            rcopy(dbuf.at[r, 0, k], drecv.at[r, 0, k], rs_s.at[r], rsd_r.at[r, 0, k], ydev(1)).start()
            rcopy(pbuf.at[r, 2, k, low], rrecv.at[r, k, low], rs_s.at[r], rsr_r.at[r, 1, k], ydev(1)).wait_recv()
            dbuf[r, 1, k, 0:64] = pbuf[r, 3, k, 0:64]
            dbuf[r, 1, k, 64:128] = (pbuf[r, 3, k, 64:128].astype(F32) + rrecv[r, k, 64:128].astype(F32)).astype(BF)
            rcopy(dbuf.at[r, 1, k], drecv.at[r, 1, k], rs_s.at[r], rsd_r.at[r, 1, k], ydev(3)).start()

    def rs_z(r):
        for k in KS:
            rcopy(dbuf.at[r, 0, k], drecv.at[r, 0, k], rs_s.at[r], rsd_r.at[r, 0, k], ydev(3)).wait_recv()
            rcopy(dbuf.at[r, 1, k], drecv.at[r, 1, k], rs_s.at[r], rsd_r.at[r, 1, k], ydev(1)).wait_recv()
            total = part(r, y, zi[k]).astype(BF).astype(F32) + drecv[r, 0, k].astype(F32) + drecv[r, 1, k].astype(F32)
            if k:
                zbuf[r, k - 1] = total.astype(BF)
                rcopy(zbuf.at[r, k - 1], zrecv.at[r, k - 1], rs_s.at[r], rsz_r.at[r, k - 1], zdev(k)).start()
            else:
                zown[r] = total

    def rs_fin(r):
        for k in (1, 3, 2):
            rcopy(zbuf.at[r, k - 1], zrecv.at[r, k - 1], rs_s.at[r], rsz_r.at[r, k - 1], zdev(4 - k)).wait_recv()
        return (
            zown[r] + zrecv[r, 0].astype(F32) + zrecv[r, 1].astype(F32) + zrecv[r, 2].astype(F32)
        )

    def forward_end(tick):
        total = rs_fin(RF1 if tick else RF0)
        ostage[tick] = (ag[X1 if tick else X0, own].astype(F32) + total).astype(BF)
        pltpu.make_async_copy(ostage.at[tick], out_all.at[0, tick], o_s.at[tick]).start()

    def backward_end(tick, mean, inv):
        total = rs_fin(RB1 if tick else RB0)
        m1, m2 = stats_end(tick)
        std = (ag[H1 if tick else H0, own].astype(F32) - mean) * inv
        grad = inv * (total * gain[:, my_cols] - m1 - std * m2)
        ostage[2 + tick] = (ag[U1 if tick else U0, own].astype(F32) + grad).astype(BF)
        pltpu.make_async_copy(ostage.at[2 + tick], out_all.at[1, tick], o_s.at[2 + tick]).start()

    def hop_copy(slot, a, forward, k):
        to = nxt if forward else prv
        recv = agz_r.at[a, k - 1] if k else hop_r.at[slot // 2]
        return rcopy(ostage.at[slot], ag.at[a, own], hop_s.at[slot // 2, k], recv, (to, zi[k] * 4 + y))

    def hop_start(slot, a, forward):
        @pl.when((s < sections - 1) if forward else (s > 0))
        def _():
            for k in (0, 1, 3, 2):
                hop_copy(slot, a, forward, k).start()

    def first_z(slot, a, k):
        return rcopy(ag.at[a, own], ag.at[a, own], fz_s.at[slot // 2, k - 1], agz_r.at[a, k - 1], zdev(k))

    def hop_wait(slot, a, forward, first):
        cp = rcopy(ostage.at[slot], ag.at[a, own], hop_s.at[slot // 2, 0], hop_r.at[slot // 2], (prv if forward else nxt, t))

        @pl.when((s > 0) if forward else (s < sections - 1))
        def _():
            cp.wait_recv()

        @pl.when((s == 0) if forward else (s == sections - 1))
        def _():
            own_copy = pltpu.make_async_copy(first, ag.at[a, own], lsem.at[slot // 2])
            own_copy.start()
            own_copy.wait()
            for k in (1, 3, 2):
                first_z(slot, a, k).start()

    def mirror_copy(tick):
        return rcopy(park.at[0, tick], prk.at[tick], m_s.at[tick], m_r.at[tick], (mir, t))

    def parked_copy(tick):
        return rcopy(pstage.at[tick], out_all.at[2, tick], m_s.at[2 + tick], m_r.at[2 + tick], (mir, t))

    def park_inflow(tick):
        mine = ag[X1 if tick else X0, own]
        pstage[tick] = jnp.where(flv[:, tick : tick + 1] == 1, mine.astype(F32), 0.0).astype(BF)
        parked_copy(tick).start()

    def choose(tick):
        mirror_copy(tick).wait_recv()
        ag[H1 if tick else H0, own] = jnp.where(
            flv[:, tick : tick + 1] == 1, prk[tick].astype(F32), stv[tick].astype(F32)
        ).astype(BF)

    mirror_copy(0).start()
    pltpu.make_async_copy(arr.at[0], ag.at[X0, own], lsem.at[0]).wait()
    ag_z(X0)
    ag_y1(X0, 0)
    pltpu.make_async_copy(agr.at[0], ag.at[U0, own], lsem.at[1]).wait()
    ag_y1(U0, 0)
    load_stash.wait()
    load_flags.wait()
    load_gain.wait()
    y1_rest(X0)
    ag_z(U0)
    choose(0)
    ag_z(H0)
    ag_y1(H0, 0)
    load_wq.wait()
    load_wo.wait()
    g_hi = gain[...].astype(BF)
    g_lo = (gain[...] - g_hi.astype(F32)).astype(BF)
    sub = lax.broadcasted_iota(jnp.int32, (16, 128), 0)
    for c in range(feats // 128):
        hi, lo = g_hi[:, c * 128 : (c + 1) * 128].astype(F32), g_lo[:, c * 128 : (c + 1) * 128].astype(F32)
        normed[0:16, c * 128 : (c + 1) * 128] = jnp.where(sub == 0, hi, jnp.where(sub == 1, lo, 0.0)).astype(BF)

    def wg_tile(n, carry):
        nn = pl.ds(pl.multiple_of(n * 256, 256), 256)
        wgs[:, nn] = jnp.sum(dot(normed[0:16, :], wq[:, nn]), axis=0, keepdims=True)
        return carry

    lax.fori_loop(0, 3, wg_tile, 0)
    y2_all(X0)
    y1_rest(U0)
    mirror_copy(1).start()
    y1_rest(H0)
    y2_all(U0)
    ag_fin(X0)
    layer_norm(X0)
    qkv()
    attended(attention())
    y2_all(H0)
    rs_o(RF0)
    grad_att3(U0)
    ag_fin(U0)
    grad_att1(U0)
    rs_d(RF0)
    ag_fin(H0)
    mean0, inv0 = layer_norm(H0)
    rs_z(RF0)
    qkv()
    heads = attention()
    choose(1)
    attend_back(heads)
    stats_start(0)
    rs_o(RB0)
    forward_end(0)
    hop_start(0, X1, True)
    ag_z(H1)
    stats_mid(0)
    rs_d(RB0)
    ag_y1(H1, 0)
    hop_wait(0, X1, True, ent.at[1])
    ag_y1(X1, 0)
    y1_rest(H1)
    rs_z(RB0)
    y1_rest(X1)
    y2_all(H1)
    backward_end(0, mean0, inv0)
    hop_start(2, U1, False)
    y2_all(X1)
    park_inflow(0)
    ag_fin(H1)
    mean1, inv1 = layer_norm(H1)
    hop_wait(2, U1, False, cot.at[1])
    ag_y1(U1, 0)
    qkv()
    heads = attention()
    p1[...] = proj[...]
    y1_rest(U1)
    ag_fin(X1)
    layer_norm(X1)
    y2_all(U1)
    qkv()
    attended(attention())
    rs_o(RF1)
    park_inflow(1)
    grad_att3(U1)
    rs_d(RF1)
    ag_fin(U1)
    grad_att1(U1)
    attend_back(heads)
    proj[...] = p1[...]
    stats_start(1)
    rs_o(RB1)
    rs_z(RF1)
    rs_d(RB1)
    stats_mid(1)
    forward_end(1)
    rs_z(RB1)
    backward_end(1, mean1, inv1)

    for a in range(6):
        sent = pl.ds(0, 12 if a in (X1, U1) else 15)
        pltpu.make_async_copy(ag.at[a, sent], ag.at[a, sent], ag_s.at[a]).wait()
    for r in range(4):
        pltpu.make_async_copy(ag.at[0, pl.ds(0, 15)], ag.at[0, pl.ds(0, 15)], rs_s.at[r]).wait()
    for tick in range(2):
        mirror_copy(tick).wait_send()
        parked_copy(tick).wait()
        pltpu.make_async_copy(ostage.at[tick], out_all.at[0, tick], o_s.at[tick]).wait()
        pltpu.make_async_copy(ostage.at[2 + tick], out_all.at[1, tick], o_s.at[2 + tick]).wait()

    for slot, a, forward in ((0, X1, True), (2, U1, False)):

        @pl.when((s < sections - 1) if forward else (s > 0))
        def _():
            for k in range(4):
                hop_copy(slot, a, forward, k).wait_send()

        @pl.when((s == 0) if forward else (s == sections - 1))
        def _():
            for k in (1, 2, 3):
                first_z(slot, a, k).wait_send()


def on_device(entering, arriving, stashed, parked, evict, cotangent, arriving_grad, qkv_weight, out_weight, norm_gain):
    any_spec = pl.BlockSpec(memory_space=pl.ANY)
    piece = lambda *lead: pltpu.VMEM(tuple(lead) + (128, 256), BF)
    dma = lambda *shape: pltpu.SemaphoreType.DMA(shape)
    slab = jax.ShapeDtypeStruct((3, 2, 128, 256), BF)
    made = pl.pallas_call(
        kernel,
        out_shape=slab,
        in_specs=[any_spec] * 10,
        out_specs=any_spec,
        scratch_shapes=[
            pltpu.VMEM(qkv_weight.shape[1:], BF),
            pltpu.VMEM(out_weight.shape[1:], BF),
            pltpu.VMEM(norm_gain.shape, F32),
            pltpu.VMEM((128, 768), F32),
            pltpu.VMEM((128, 256), F32),
            piece(2),
            piece(2),
            pltpu.VMEM((1, 2), jnp.int32),
            piece(6, 16),
            pltpu.VMEM((128, 4096), BF),
            pltpu.VMEM((128, 768), F32),
            pltpu.VMEM((128, 256), BF),
            pltpu.VMEM((128, 256), BF),
            pltpu.VMEM((128, 768), BF),
            pltpu.VMEM((1, 768), F32),
            piece(4, 4, 4),
            piece(4, 2, 4),
            piece(4, 3),
            piece(4, 4),
            piece(4, 2, 4),
            piece(4, 3),
            pltpu.VMEM((4, 128, 256), F32),
            pltpu.VMEM((2, 8, 128), F32),
            pltpu.VMEM((2, 3, 8, 128), F32),
            pltpu.VMEM((2, 8, 128), F32),
            pltpu.VMEM((2, 3, 8, 128), F32),
            piece(4),
            piece(2),
            dma(7),
            dma(6),
            dma(6, 3),
            dma(6, 4, 4),
            dma(4),
            dma(4, 2, 4),
            dma(4, 2, 4),
            dma(4, 3),
            dma(2, 6),
            dma(2, 6),
            dma(4),
            dma(4),
            dma(2, 4),
            dma(2),
            dma(2, 3),
            dma(4),
        ],
        compiler_params=pltpu.CompilerParams(
            collective_id=0, has_side_effects=True, vmem_limit_bytes=56 * 2**20
        ),
        cost_estimate=pl.CostEstimate(flops=6 * 10**9, bytes_accessed=10**7, transcendentals=10**5),
        name="relay_window",
    )(entering, arriving, stashed, parked, evict, cotangent, arriving_grad, qkv_weight, out_weight, norm_gain)

    return made[0:1], made[1:2], made[2:3]


def solution(mesh):
    in_specs = (
        P(None, None, "tensor"),
        P("section", None, "tensor"),
        P("section", None, None, "tensor"),
        P("section", None, None, "tensor"),
        P("section", None),
        P(None, None, "tensor"),
        P("section", None, "tensor"),
        P("section", None, "tensor"),
        P("section", "tensor", None),
        P("section", None),
    )
    out_specs = (P("section", None, None, "tensor"),) * 3
    return jax.shard_map(on_device, mesh=mesh, in_specs=in_specs, out_specs=out_specs, check_vma=False)
```

```python
import functools
import math

import jax
import jax.numpy as jnp
from jax import lax
from jax.experimental import pallas as pl
from jax.experimental.pallas import tpu as pltpu
from jax.sharding import PartitionSpec as P

MESH = pl.DeviceIdType.MESH
HD = 128
BF = jnp.bfloat16
F32 = jnp.float32

X0, U0, H0, H1, X1, U1 = range(6)
RF0, RB0, RF1, RB1 = range(4)


def dot(a, b):
    return lax.dot_general(a, b, (((1,), (0,)), ((), ())), preferred_element_type=F32)


def dot_nt(a, b):
    return lax.dot_general(a, b, (((1,), (1,)), ((), ())), preferred_element_type=F32)


def dot_tn(a, b):
    return lax.dot_general(a, b, (((0,), (0,)), ((), ())), preferred_element_type=F32)


def kernel(
    ent, arr, stash, park, flags, cot, agr, wq_h, wo_h, gain_h,
    out_all,
    wq, wo, gain, p1, gaf, stv, prk, flv, ag, normed, proj, att, gab, gpb, wgs,
    pbuf, dbuf, zbuf, rrecv, drecv, zrecv, zown, sbuf, srecv, szbuf, szrecv, ostage, pstage,
    lsem, ag_s, agz_r, agy_r, rs_s, rsr_r, rsd_r, rsz_r, st_s, st_r, m_s, m_r, hop_s, hop_r, fz_s, o_s,
):
    s, t = lax.axis_index("section"), lax.axis_index("tensor")
    sections = lax.axis_size("section")
    y, z = lax.rem(t, 4), lax.div(t, 4)
    yi = [y, lax.rem(y + 1, 4), lax.rem(y + 2, 4), lax.rem(y + 3, 4)]
    zi = [z, lax.rem(z + 1, 4), lax.rem(z + 2, 4), lax.rem(z + 3, 4)]
    nxt, prv = lax.rem(s + 1, sections), lax.rem(s + sections - 1, sections)
    mir = sections - 1 - s
    ydev = lambda j: (s, z * 4 + yi[j])
    zdev = lambda k: (s, zi[k] * 4 + y)
    feats = normed.shape[1]

    def chunk(yy, zz):
        return yy * 4 + zz

    def cols(yy, zz):
        return pl.ds(pl.multiple_of((zz * 4 + yy) * 256, 256), 256)

    own = chunk(y, z)
    my_cols = cols(y, z)

    def rcopy(src, dst, ss, rs, dev):
        return pltpu.make_async_remote_copy(
            src_ref=src, dst_ref=dst, send_sem=ss, recv_sem=rs, device_id=dev, device_id_type=MESH
        )

    @pl.when(s == 0)
    def _():
        pltpu.make_async_copy(ent.at[0], ag.at[X0, own], lsem.at[0]).start()

    @pl.when(s > 0)
    def _():
        pltpu.make_async_copy(arr.at[0], ag.at[X0, own], lsem.at[0]).start()

    @pl.when(s == sections - 1)
    def _():
        pltpu.make_async_copy(cot.at[0], ag.at[U0, own], lsem.at[1]).start()

    @pl.when(s < sections - 1)
    def _():
        pltpu.make_async_copy(agr.at[0], ag.at[U0, own], lsem.at[1]).start()

    load_stash = pltpu.make_async_copy(stash.at[0], stv, lsem.at[2])
    load_stash.start()
    load_flags = pltpu.make_async_copy(flags, flv, lsem.at[6])
    load_flags.start()
    load_gain = pltpu.make_async_copy(gain_h, gain, lsem.at[3])
    load_gain.start()
    load_wq = pltpu.make_async_copy(wq_h.at[0], wq, lsem.at[4])
    load_wq.start()
    load_wo = pltpu.make_async_copy(wo_h.at[0], wo, lsem.at[5])
    load_wo.start()

    barrier = pltpu.get_barrier_semaphore()
    peers = [ydev(1), ydev(2), ydev(3), zdev(1), zdev(2), zdev(3), (mir, t)]
    peers += [(sec, zi[k] * 4 + y) for sec in (nxt, prv) for k in range(4)]
    for dev in peers:
        pl.semaphore_signal(barrier, inc=1, device_id=dev, device_id_type=MESH)
    pl.semaphore_wait(barrier, len(peers))

    def gz_copy(a, k):
        return rcopy(ag.at[a, own], ag.at[a, own], ag_s.at[a], agz_r.at[a, k - 1], zdev(k))

    def gz_wait(a, k):
        c = chunk(y, zi[(4 - k) % 4])
        rcopy(ag.at[a, c], ag.at[a, c], ag_s.at[a], agz_r.at[a, k - 1], zdev((4 - k) % 4)).wait_recv()

    def ag_z(a):
        for k in (1, 3, 2):
            gz_copy(a, k).start()

    def ag_y1(a, k):
        c = chunk(y, zi[(4 - k) % 4])
        if k:
            gz_wait(a, k)
        rcopy(ag.at[a, c], ag.at[a, c], ag_s.at[a], agy_r.at[a, 0, k], ydev(1)).start()
        rcopy(ag.at[a, c], ag.at[a, c], ag_s.at[a], agy_r.at[a, 1, k], ydev(3)).start()

    def ag_y2(a, k):
        zz = zi[(4 - k) % 4]
        c = chunk(yi[3], zz)
        rcopy(ag.at[a, c], ag.at[a, c], ag_s.at[a], agy_r.at[a, 0, k], ydev(3)).wait_recv()
        top = ag.at[a, c, pl.ds(0, 64)]
        rcopy(top, top, ag_s.at[a], agy_r.at[a, 2, k], ydev(1)).start()
        c = chunk(yi[1], zz)
        rcopy(ag.at[a, c], ag.at[a, c], ag_s.at[a], agy_r.at[a, 1, k], ydev(1)).wait_recv()
        low = ag.at[a, c, pl.ds(64, 64)]
        rcopy(low, low, ag_s.at[a], agy_r.at[a, 3, k], ydev(3)).start()

    def ag_fin(a):
        for k in (0, 1, 3, 2):
            c = chunk(yi[2], zi[(4 - k) % 4])
            top, low = ag.at[a, c, pl.ds(0, 64)], ag.at[a, c, pl.ds(64, 64)]
            rcopy(top, top, ag_s.at[a], agy_r.at[a, 2, k], ydev(3)).wait_recv()
            rcopy(low, low, ag_s.at[a], agy_r.at[a, 3, k], ydev(1)).wait_recv()

    def y1_rest(a):
        for k in (1, 3, 2):
            ag_y1(a, k)

    def y2_all(a):
        for k in (0, 1, 3, 2):
            ag_y2(a, k)

    def layer_norm(a):
        def add(c, acc):
            return acc + ag[a, c].astype(F32)

        acc = lax.fori_loop(0, 16, add, jnp.zeros((128, 256), F32), unroll=4)
        mean = jnp.sum(acc, axis=1, keepdims=True) * (1.0 / feats)

        def var(c, acc):
            d = ag[a, c].astype(F32) - mean
            return acc + d * d

        acc = lax.fori_loop(0, 16, var, jnp.zeros((128, 256), F32), unroll=4)
        inv = lax.rsqrt(jnp.sum(acc, axis=1, keepdims=True) * (1.0 / feats) + 1e-05)

        def put(c, carry):
            cc = cols(lax.div(c, 4), lax.rem(c, 4))
            normed[:, cc] = ((ag[a, c].astype(F32) - mean) * inv * gain[:, cc]).astype(BF)
            return carry

        lax.fori_loop(0, 16, put, 0, unroll=4)
        return mean, inv

    def qkv():
        def tile(n, carry):
            nn = pl.ds(pl.multiple_of(n * 256, 256), 256)
            proj[:, nn] = dot(normed[...], wq[:, nn])
            return carry

        lax.fori_loop(0, 3, tile, 0, unroll=3)

    scale = 1.0 / math.sqrt(HD)

    def attention():
        rows = lax.broadcasted_iota(jnp.int32, (128, 128), 0)
        lanes = lax.broadcasted_iota(jnp.int32, (128, 128), 1)
        out = []
        for h in range(2):
            q, k, v = (proj[:, h * 384 + i * 128 : h * 384 + (i + 1) * 128].astype(BF) for i in range(3))
            e = jnp.where(lanes <= rows, jnp.exp(dot_nt(q, k) * scale), 0.0)
            p = e / jnp.sum(e, axis=1, keepdims=True)
            out.append((q, k, v, p, p.astype(BF)))
        return out

    def attended(heads):
        for h, (q, k, v, p, w) in enumerate(heads):
            att[:, h * 128 : (h + 1) * 128] = dot(w, v).astype(BF)

    def grad_cols(a, js, first):
        acc = first
        for j in js:

            def step(zz, acc, j=j):
                return acc + dot_nt(ag[a, chunk(yi[j], zz)], wo[:, cols(yi[j], zz)])

            acc = lax.fori_loop(0, 4, step, acc, unroll=4)
        return acc

    def grad_att3(a):
        gaf[...] = grad_cols(a, (0, 1, 3), jnp.zeros((128, 256), F32))

    def grad_att1(a):
        gab[...] = grad_cols(a, (2,), gaf[...]).astype(BF)

    def attend_back(heads):
        for h, (q, k, v, p, w) in enumerate(heads):
            ga = gab[:, h * 128 : (h + 1) * 128]
            gv = dot_tn(w, ga).astype(BF)
            g = dot_nt(ga, v)
            gs = (p * (g - jnp.sum(p * g, axis=1, keepdims=True)) * scale).astype(BF)
            gpb[:, h * 384 : h * 384 + 128] = dot(gs, k).astype(BF)
            gpb[:, h * 384 + 128 : h * 384 + 256] = dot_tn(gs, q).astype(BF)
            gpb[:, h * 384 + 256 : h * 384 + 384] = gv

    def stats_start(tick):
        g = gpb[...].astype(F32)
        s1 = jnp.sum(g * wgs[...], axis=1, keepdims=True)
        s2 = jnp.sum(g * proj[...], axis=1, keepdims=True)
        lanes = lax.broadcasted_iota(jnp.int32, (128, 128), 1)
        both = jnp.where(lanes == 0, s1, jnp.where(lanes == 1, s2, 0.0))
        sbuf[tick] = both.T[0:8]
        for j in (1, 2, 3):
            rcopy(sbuf.at[tick], srecv.at[tick, j - 1], st_s.at[tick, j - 1], st_r.at[tick, j - 1], ydev(j)).start()

    def stats_mid(tick):
        for j in (1, 2, 3):
            rcopy(sbuf.at[tick], srecv.at[tick, j - 1], st_s.at[tick, j - 1], st_r.at[tick, j - 1], ydev(4 - j)).wait()
        szbuf[tick] = sbuf[tick] + srecv[tick, 0] + srecv[tick, 1] + srecv[tick, 2]
        for k in (1, 2, 3):
            rcopy(szbuf.at[tick], szrecv.at[tick, k - 1], st_s.at[tick, k + 2], st_r.at[tick, k + 2], zdev(k)).start()

    def stats_end(tick):
        for k in (1, 2, 3):
            rcopy(szbuf.at[tick], szrecv.at[tick, k - 1], st_s.at[tick, k + 2], st_r.at[tick, k + 2], zdev(4 - k)).wait()
        total = szbuf[tick] + szrecv[tick, 0] + szrecv[tick, 1] + szrecv[tick, 2]
        back = jnp.concatenate([total, jnp.zeros((120, 128), F32)], axis=0).T
        return back[:, 0:1] * (1.0 / feats), back[:, 1:2] * (1.0 / feats)

    KS = (1, 3, 2, 0)

    def part(r, yy, zz):
        if r in (RF0, RF1):
            return dot(att[...], wo[:, cols(yy, zz)])
        return dot_nt(gpb[...], wq[cols(yy, zz), :])

    def rs_o(r):
        for k in KS:
            pbuf[r, 2, k] = part(r, yi[2], zi[k]).astype(BF)
            top, low = pl.ds(0, 64), pl.ds(64, 64)
            rcopy(pbuf.at[r, 2, k, top], rrecv.at[r, k, top], rs_s.at[r], rsr_r.at[r, 0, k], ydev(1)).start()
            rcopy(pbuf.at[r, 2, k, low], rrecv.at[r, k, low], rs_s.at[r], rsr_r.at[r, 1, k], ydev(3)).start()
        for k in KS:
            pbuf[r, 1, k] = part(r, yi[1], zi[k]).astype(BF)
            pbuf[r, 3, k] = part(r, yi[3], zi[k]).astype(BF)

    def rs_d(r):
        top, low = pl.ds(0, 64), pl.ds(64, 64)
        for k in KS:
            rcopy(pbuf.at[r, 2, k, top], rrecv.at[r, k, top], rs_s.at[r], rsr_r.at[r, 0, k], ydev(3)).wait_recv()
            dbuf[r, 0, k, 0:64] = (pbuf[r, 1, k, 0:64].astype(F32) + rrecv[r, k, 0:64].astype(F32)).astype(BF)
            dbuf[r, 0, k, 64:128] = pbuf[r, 1, k, 64:128]
            rcopy(dbuf.at[r, 0, k], drecv.at[r, 0, k], rs_s.at[r], rsd_r.at[r, 0, k], ydev(1)).start()
            rcopy(pbuf.at[r, 2, k, low], rrecv.at[r, k, low], rs_s.at[r], rsr_r.at[r, 1, k], ydev(1)).wait_recv()
            dbuf[r, 1, k, 0:64] = pbuf[r, 3, k, 0:64]
            dbuf[r, 1, k, 64:128] = (pbuf[r, 3, k, 64:128].astype(F32) + rrecv[r, k, 64:128].astype(F32)).astype(BF)
            rcopy(dbuf.at[r, 1, k], drecv.at[r, 1, k], rs_s.at[r], rsd_r.at[r, 1, k], ydev(3)).start()

    def rs_z(r):
        for k in KS:
            rcopy(dbuf.at[r, 0, k], drecv.at[r, 0, k], rs_s.at[r], rsd_r.at[r, 0, k], ydev(3)).wait_recv()
            rcopy(dbuf.at[r, 1, k], drecv.at[r, 1, k], rs_s.at[r], rsd_r.at[r, 1, k], ydev(1)).wait_recv()
            total = part(r, y, zi[k]).astype(BF).astype(F32) + drecv[r, 0, k].astype(F32) + drecv[r, 1, k].astype(F32)
            if k:
                zbuf[r, k - 1] = total.astype(BF)
                rcopy(zbuf.at[r, k - 1], zrecv.at[r, k - 1], rs_s.at[r], rsz_r.at[r, k - 1], zdev(k)).start()
            else:
                zown[r] = total

    def rs_fin(r):
        for k in (1, 3, 2):
            rcopy(zbuf.at[r, k - 1], zrecv.at[r, k - 1], rs_s.at[r], rsz_r.at[r, k - 1], zdev(4 - k)).wait_recv()
        return (
            zown[r] + zrecv[r, 0].astype(F32) + zrecv[r, 1].astype(F32) + zrecv[r, 2].astype(F32)
        )

    def forward_end(tick):
        total = rs_fin(RF1 if tick else RF0)
        ostage[tick] = (ag[X1 if tick else X0, own].astype(F32) + total).astype(BF)
        pltpu.make_async_copy(ostage.at[tick], out_all.at[0, tick], o_s.at[tick]).start()

    def backward_end(tick, mean, inv):
        total = rs_fin(RB1 if tick else RB0)
        m1, m2 = stats_end(tick)
        std = (ag[H1 if tick else H0, own].astype(F32) - mean) * inv
        grad = inv * (total * gain[:, my_cols] - m1 - std * m2)
        ostage[2 + tick] = (ag[U1 if tick else U0, own].astype(F32) + grad).astype(BF)
        pltpu.make_async_copy(ostage.at[2 + tick], out_all.at[1, tick], o_s.at[2 + tick]).start()

    def hop_copy(slot, a, forward, k):
        to = nxt if forward else prv
        recv = agz_r.at[a, k - 1] if k else hop_r.at[slot // 2]
        return rcopy(ostage.at[slot], ag.at[a, own], hop_s.at[slot // 2, k], recv, (to, zi[k] * 4 + y))

    def hop_start(slot, a, forward):
        @pl.when((s < sections - 1) if forward else (s > 0))
        def _():
            for k in (0, 1, 3, 2):
                hop_copy(slot, a, forward, k).start()

    def first_z(slot, a, k):
        return rcopy(ag.at[a, own], ag.at[a, own], fz_s.at[slot // 2, k - 1], agz_r.at[a, k - 1], zdev(k))

    def hop_wait(slot, a, forward, first):
        cp = rcopy(ostage.at[slot], ag.at[a, own], hop_s.at[slot // 2, 0], hop_r.at[slot // 2], (prv if forward else nxt, t))

        @pl.when((s > 0) if forward else (s < sections - 1))
        def _():
            cp.wait_recv()

        @pl.when((s == 0) if forward else (s == sections - 1))
        def _():
            own_copy = pltpu.make_async_copy(first, ag.at[a, own], lsem.at[slot // 2])
            own_copy.start()
            own_copy.wait()
            for k in (1, 3, 2):
                first_z(slot, a, k).start()

    def mirror_copy(tick):
        return rcopy(park.at[0, tick], prk.at[tick], m_s.at[tick], m_r.at[tick], (mir, t))

    def parked_copy(tick):
        return rcopy(pstage.at[tick], out_all.at[2, tick], m_s.at[2 + tick], m_r.at[2 + tick], (mir, t))

    def park_inflow(tick):
        mine = ag[X1 if tick else X0, own]
        pstage[tick] = jnp.where(flv[:, tick : tick + 1] == 1, mine.astype(F32), 0.0).astype(BF)
        parked_copy(tick).start()

    def choose(tick):
        mirror_copy(tick).wait_recv()
        ag[H1 if tick else H0, own] = jnp.where(
            flv[:, tick : tick + 1] == 1, prk[tick].astype(F32), stv[tick].astype(F32)
        ).astype(BF)

    mirror_copy(0).start()
    pltpu.make_async_copy(arr.at[0], ag.at[X0, own], lsem.at[0]).wait()
    ag_z(X0)
    ag_y1(X0, 0)
    pltpu.make_async_copy(agr.at[0], ag.at[U0, own], lsem.at[1]).wait()
    ag_y1(U0, 0)
    load_stash.wait()
    load_flags.wait()
    load_gain.wait()
    y1_rest(X0)
    ag_z(U0)
    choose(0)
    ag_z(H0)
    ag_y1(H0, 0)
    load_wq.wait()
    load_wo.wait()
    g_hi = gain[...].astype(BF)
    g_lo = (gain[...] - g_hi.astype(F32)).astype(BF)
    sub = lax.broadcasted_iota(jnp.int32, (16, 128), 0)
    for c in range(feats // 128):
        hi, lo = g_hi[:, c * 128 : (c + 1) * 128].astype(F32), g_lo[:, c * 128 : (c + 1) * 128].astype(F32)
        normed[0:16, c * 128 : (c + 1) * 128] = jnp.where(sub == 0, hi, jnp.where(sub == 1, lo, 0.0)).astype(BF)

    def wg_tile(n, carry):
        nn = pl.ds(pl.multiple_of(n * 256, 256), 256)
        wgs[:, nn] = jnp.sum(dot(normed[0:16, :], wq[:, nn]), axis=0, keepdims=True)
        return carry

    lax.fori_loop(0, 3, wg_tile, 0)
    y2_all(X0)
    y1_rest(U0)
    mirror_copy(1).start()
    y1_rest(H0)
    y2_all(U0)
    ag_fin(X0)
    layer_norm(X0)
    qkv()
    attended(attention())
    y2_all(H0)
    rs_o(RF0)
    grad_att3(U0)
    ag_fin(U0)
    grad_att1(U0)
    rs_d(RF0)
    ag_fin(H0)
    mean0, inv0 = layer_norm(H0)
    rs_z(RF0)
    qkv()
    heads = attention()
    choose(1)
    attend_back(heads)
    stats_start(0)
    rs_o(RB0)
    forward_end(0)
    hop_start(0, X1, True)
    ag_z(H1)
    stats_mid(0)
    rs_d(RB0)
    ag_y1(H1, 0)
    hop_wait(0, X1, True, ent.at[1])
    ag_y1(X1, 0)
    y1_rest(H1)
    rs_z(RB0)
    y1_rest(X1)
    y2_all(H1)
    backward_end(0, mean0, inv0)
    hop_start(2, U1, False)
    y2_all(X1)
    park_inflow(0)
    ag_fin(H1)
    mean1, inv1 = layer_norm(H1)
    hop_wait(2, U1, False, cot.at[1])
    ag_y1(U1, 0)
    qkv()
    heads = attention()
    p1[...] = proj[...]
    y1_rest(U1)
    ag_fin(X1)
    layer_norm(X1)
    y2_all(U1)
    qkv()
    attended(attention())
    rs_o(RF1)
    park_inflow(1)
    grad_att3(U1)
    rs_d(RF1)
    ag_fin(U1)
    grad_att1(U1)
    attend_back(heads)
    proj[...] = p1[...]
    stats_start(1)
    rs_o(RB1)
    rs_z(RF1)
    rs_d(RB1)
    stats_mid(1)
    forward_end(1)
    rs_z(RB1)
    backward_end(1, mean1, inv1)

    for a in range(6):
        sent = pl.ds(0, 12 if a in (X1, U1) else 15)
        pltpu.make_async_copy(ag.at[a, sent], ag.at[a, sent], ag_s.at[a]).wait()
    for r in range(4):
        pltpu.make_async_copy(ag.at[0, pl.ds(0, 15)], ag.at[0, pl.ds(0, 15)], rs_s.at[r]).wait()
    for tick in range(2):
        mirror_copy(tick).wait_send()
        parked_copy(tick).wait()
        pltpu.make_async_copy(ostage.at[tick], out_all.at[0, tick], o_s.at[tick]).wait()
        pltpu.make_async_copy(ostage.at[2 + tick], out_all.at[1, tick], o_s.at[2 + tick]).wait()

    for slot, a, forward in ((0, X1, True), (2, U1, False)):

        @pl.when((s < sections - 1) if forward else (s > 0))
        def _():
            for k in range(4):
                hop_copy(slot, a, forward, k).wait_send()

        @pl.when((s == 0) if forward else (s == sections - 1))
        def _():
            for k in (1, 2, 3):
                first_z(slot, a, k).wait_send()


def on_device(entering, arriving, stashed, parked, evict, cotangent, arriving_grad, qkv_weight, out_weight, norm_gain):
    any_spec = pl.BlockSpec(memory_space=pl.ANY)
    piece = lambda *lead: pltpu.VMEM(tuple(lead) + (128, 256), BF)
    dma = lambda *shape: pltpu.SemaphoreType.DMA(shape)
    slab = jax.ShapeDtypeStruct((3, 2, 128, 256), BF)
    made = pl.pallas_call(
        kernel,
        out_shape=slab,
        in_specs=[any_spec] * 10,
        out_specs=any_spec,
        scratch_shapes=[
            pltpu.VMEM(qkv_weight.shape[1:], BF),
            pltpu.VMEM(out_weight.shape[1:], BF),
            pltpu.VMEM(norm_gain.shape, F32),
            pltpu.VMEM((128, 768), F32),
            pltpu.VMEM((128, 256), F32),
            piece(2),
            piece(2),
            pltpu.VMEM((1, 2), jnp.int32),
            piece(6, 16),
            pltpu.VMEM((128, 4096), BF),
            pltpu.VMEM((128, 768), F32),
            pltpu.VMEM((128, 256), BF),
            pltpu.VMEM((128, 256), BF),
            pltpu.VMEM((128, 768), BF),
            pltpu.VMEM((1, 768), F32),
            piece(4, 4, 4),
            piece(4, 2, 4),
            piece(4, 3),
            piece(4, 4),
            piece(4, 2, 4),
            piece(4, 3),
            pltpu.VMEM((4, 128, 256), F32),
            pltpu.VMEM((2, 8, 128), F32),
            pltpu.VMEM((2, 3, 8, 128), F32),
            pltpu.VMEM((2, 8, 128), F32),
            pltpu.VMEM((2, 3, 8, 128), F32),
            piece(4),
            piece(2),
            dma(7),
            dma(6),
            dma(6, 3),
            dma(6, 4, 4),
            dma(4),
            dma(4, 2, 4),
            dma(4, 2, 4),
            dma(4, 3),
            dma(2, 6),
            dma(2, 6),
            dma(4),
            dma(4),
            dma(2, 4),
            dma(2),
            dma(2, 3),
            dma(4),
        ],
        compiler_params=pltpu.CompilerParams(
            collective_id=0, has_side_effects=True, vmem_limit_bytes=56 * 2**20
        ),
        cost_estimate=pl.CostEstimate(flops=6 * 10**9, bytes_accessed=10**7, transcendentals=10**5),
        name="relay_window",
    )(entering, arriving, stashed, parked, evict, cotangent, arriving_grad, qkv_weight, out_weight, norm_gain)

    return made[0:1], made[1:2], made[2:3]


def solution(mesh):
    in_specs = (
        P(None, None, "tensor"),
        P("section", None, "tensor"),
        P("section", None, None, "tensor"),
        P("section", None, None, "tensor"),
        P("section", None),
        P(None, None, "tensor"),
        P("section", None, "tensor"),
        P("section", None, "tensor"),
        P("section", "tensor", None),
        P("section", None),
    )
    out_specs = (P("section", None, None, "tensor"),) * 3
    return jax.shard_map(on_device, mesh=mesh, in_specs=in_specs, out_specs=out_specs, check_vma=False)
```
